512 devices in a mesh: dp: 8 (over y), seq: 64 (over z, x, core).
Axes of the slice: x: 4, y: 8, z: 8, core: 2. Of those that a mesh axis runs over, the one named last changes fastest.
Arguments:
- tokens: bfloat16 [8, 32768, 1024], P('dp', 'seq'), may hold values from -50 to 50
- w_query: bfloat16 [1024, 1024], P(None, 'dp'), may hold values from -0.1875 to 0.1875
- w_key: bfloat16 [1024, 1024], P(None, 'dp'), may hold values from -0.1875 to 0.1875
- w_value: bfloat16 [1024, 1024], P(None, 'dp'), may hold values from -0.1875 to 0.1875
- w_out: bfloat16 [1024, 1024], P('dp'), may hold values from -0.1875 to 0.1875
- norm_gain: float32 [1024], replicated, may hold values from 0.1 to 1.9
Outputs:
- layer_out: bfloat16 [8, 32768, 1024], P('dp', 'seq')
The draws below stay inside these ranges and needn't reach their ends.
All inputs are finite; a program needn't handle non-finite values.
Results may differ from the reference program's by a relative error of at most 0.017.
Values may be sent and summed in bfloat16 or wider, within the bound.
No kernel may reach another device: no remote copies, remote signals or barrier semaphores. Data moves between devices by JAX's collectives and lax.ppermute only.
A program may use at most 128 MiB of HBM per device.

```python
import math
import jax
import jax.numpy as jnp
from jax import lax

D = 1024
H = 8
DH = 128
TOK_DEV = 512
STACKS = 8
SEQ = 32768


def draw_tokens(key, part):
    first, second, third = jax.random.split(jax.random.fold_in(key, 11), 3)
    base = jnp.clip(jax.random.normal(first, (STACKS, SEQ, D), jnp.float32), -4.0, 4.0)
    row_scale = jnp.exp(jax.random.uniform(second, (STACKS, SEQ, 1), jnp.float32, 0.0, math.log(10.0)))
    col_scale = jnp.exp(jax.random.uniform(third, (D,), jnp.float32, 0.0, math.log(10.0)))
    return (base * row_scale * col_scale * 0.1).astype(jnp.bfloat16)


def steps_of(rng, extent, cuts, low, top_value):
    def one(dim, blocks):
        steps = jax.random.uniform(jax.random.fold_in(jax.random.fold_in(rng, 6), dim), (blocks,), jnp.float32, low / len(cuts), top_value / len(cuts))
        return jnp.repeat(jnp.exp(steps), extent[dim] // blocks).reshape((-1,) + (1,) * (len(extent) - dim - 1))

    level = one(*cuts[0])
    for cut in cuts[1:]:
        level = level * one(*cut)
    return level


def scatter_about(own_key, dims, spread, limit, cuts=(), kind=jnp.bfloat16):
    result = spread * jax.random.normal(own_key, dims, jnp.float32)
    if cuts:
        result = result * steps_of(own_key, dims, cuts, -0.22, 0.18)
    return jnp.clip(result, -limit, limit).astype(kind)


def setup_inputs(seed: int = 0) -> dict:
    key_of = jax.random.split(jax.random.key(seed), 7)
    tokens = draw_tokens(jax.random.fold_in(key_of[6], 71), 0)
    w_query = scatter_about(key_of[1], (D, D), D ** -0.5, 0.1875, ((1, 8),))
    w_key = scatter_about(key_of[2], (D, D), D ** -0.5, 0.1875, ((1, 8),))
    w_value = scatter_about(key_of[3], (D, D), D ** -0.5, 0.1875, ((1, 8),))
    w_out = scatter_about(key_of[4], (D, D), D ** -0.5, 0.1875, ((0, 8),))
    norm_gain = jnp.clip(1.0 + 0.18 * jax.random.normal(key_of[5], (D,), jnp.float32), 0.1, 1.9)
    return {"tokens": tokens, "w_query": w_query, "w_key": w_key, "w_value": w_value, "w_out": w_out, "norm_gain": norm_gain}


def rounded(value):
    return lax.optimization_barrier(value.astype(jnp.bfloat16)).astype(jnp.float32)

def inner_block(query_heads, key_heads, value_heads):
    length = query_heads.shape[1]
    block = min(length, 512)
    pieces = []
    for begin in range(0, length, block):
        finish = begin + block
        scores = jnp.einsum('hid,hjd->hij', query_heads[:, begin:finish].astype(jnp.float32), key_heads[:, :finish].astype(jnp.float32))
        row_ids = jnp.arange(begin, finish)[:, None]
        col_ids = jnp.arange(finish)[None, :]
        scores = rounded(jnp.where(col_ids <= row_ids, scores, 0.0))
        pieces.append(jnp.einsum('hij,hje->hie', scores, value_heads[:, :finish].astype(jnp.float32)))
    return jnp.concatenate(pieces, axis=1)

def reference(tokens, w_query, w_key, w_value, w_out, norm_gain):
    gain_heads = norm_gain.reshape(H, 1, DH)

    def one_stack(rows):

        def heads(weight):
            proj = jnp.dot(rows, weight, preferred_element_type=jnp.float32).astype(jnp.bfloat16)
            return proj.reshape(SEQ // TOK_DEV, TOK_DEV, H, DH).transpose(0, 2, 1, 3)
        blocks = (heads(w_query), heads(w_key), heads(w_value))

        def step(state, block):
            query_heads, key_heads, value_heads = block
            carried = jnp.einsum('htd,hde->hte', query_heads.astype(jnp.float32), rounded(state))
            mixed_raw = inner_block(query_heads, key_heads, value_heads) + carried
            scale = lax.rsqrt(lax.optimization_barrier(jnp.mean(mixed_raw * mixed_raw, axis=-1, keepdims=True)) + 1e-05)
            normed = (mixed_raw * scale * gain_heads).astype(jnp.bfloat16)
            state = state + jnp.einsum('htd,hte->hde', key_heads.astype(jnp.float32), value_heads.astype(jnp.float32))
            return (state, normed)
        start_state = jnp.zeros((H, DH, DH), jnp.float32)
        _, normed = lax.scan(step, start_state, blocks)
        normed = normed.transpose(0, 2, 1, 3).reshape(SEQ, D)
        return jnp.dot(normed, w_out, preferred_element_type=jnp.float32).astype(jnp.bfloat16)
    return lax.map(one_stack, tokens)
```

```python
import jax
import jax.numpy as jnp
from jax import lax
from jax.experimental import pallas as pl
from jax.experimental.pallas import tpu as pltpu
from jax.sharding import Mesh
from jax.sharding import PartitionSpec as P


DP, ZN, XN = 8, 8, 4
CHIPS = ZN * XN
TOK = 512
D = 1024
DH = 128
SLOTS = 4
F32 = jnp.float32
BF16 = jnp.bfloat16
SWAP = [(0, 1), (1, 0)]
VMEM = pl.BlockSpec(memory_space=pltpu.VMEM)
HBM = pl.BlockSpec(memory_space=pl.ANY)


def toward(distance):
    pairs = []
    for y in range(DP):
        for place in range(2 * CHIPS):
            step = -distance if place % 2 == 0 else distance
            pairs.append((y * 2 * CHIPS + place, (y + step) % DP * 2 * CHIPS + place))
    return pairs


def hop(weight, distance):
    return lax.ppermute(weight, ("dp", "z", "x", "core"), toward(distance))


def call(kernel, outs, flops, moved, specs=None, scratch=(), count=None):
    return pl.pallas_call(
        kernel,
        out_shape=outs,
        in_specs=specs if specs is not None else [VMEM] * count,
        out_specs=jax.tree.map(lambda _: VMEM, outs),
        scratch_shapes=list(scratch),
        compiler_params=pltpu.CompilerParams(vmem_limit_bytes=32 * 1024 * 1024),
        cost_estimate=pl.CostEstimate(flops=flops, bytes_accessed=moved, transcendentals=0),
    )


def shape(dims, kind):
    return jax.ShapeDtypeStruct(dims, kind)


def mm(a, b):
    return jnp.dot(a, b, preferred_element_type=F32)


def mm_t(a, b):
    return lax.dot_general(a, b, (((1,), (1,)), ((), ())), preferred_element_type=F32)


def t_mm(a, b):
    return lax.dot_general(a, b, (((0,), (0,)), ((), ())), preferred_element_type=F32)


def project(tokens_refs, weight, key_ref, value_ref, state_ref):
    for block, tokens_ref in enumerate(tokens_refs):
        both = mm(tokens_ref[...], weight).astype(BF16)
        key, value = both[:, :DH], both[:, DH:]
        key_ref[block] = key
        value_ref[block] = value
        state_ref[block] = t_mm(key, value)


def key_value_kernel(own_ref, other_ref, wk_ref, wv_ref, key_ref, value_ref, state_ref):
    weight = jnp.concatenate([wk_ref[...], wv_ref[...]], axis=1)
    project((own_ref, other_ref), weight, key_ref, value_ref, state_ref)


def last_key_value_kernel(
    own_ref, other_ref, wk_ref, wv_ref, wk_far_ref, wv_far_ref, s0, s1, s2, key_ref, value_ref, state_ref, total_ref
):
    first = lax.axis_index("core") == 0
    wk = jnp.where(first, wk_ref[...], wk_far_ref[...])
    wv = jnp.where(first, wv_ref[...], wv_far_ref[...])
    project((own_ref, other_ref), jnp.concatenate([wk, wv], axis=1), key_ref, value_ref, state_ref)
    for slot, ref in enumerate((s0, s1, s2, state_ref)):
        total_ref[slot] = (ref[0] + ref[1]).astype(BF16)


def within_kernel(own_ref, other_ref, q0, q1, q2, q_own, q_far, k0, k1, k2, k3, v0, v1, v2, v3, query_ref, within_ref):
    first = lax.axis_index("core") == 0
    wq3 = jnp.where(first, q_own[...], q_far[...])
    weights = (
        jnp.concatenate([q0[...], q1[...]], axis=1),
        jnp.concatenate([q2[...], wq3], axis=1),
    )
    keys, values = (k0, k1, k2, k3), (v0, v1, v2, v3)
    half = TOK // 2
    rows = lax.broadcasted_iota(jnp.int32, (half, half), 0)
    cols = lax.broadcasted_iota(jnp.int32, (half, half), 1)
    keep = cols <= rows
    for block, tokens_ref in enumerate((own_ref, other_ref)):
        for pair in range(2):
            both = mm(tokens_ref[...], weights[pair]).astype(BF16)
            for side in range(2):
                slot = 2 * pair + side
                query = both[:, side * DH : (side + 1) * DH]
                query_ref[slot, block] = query
                key, value = keys[slot][block], values[slot][block]
                top = jnp.where(keep, mm_t(query[:half], key[:half]), 0.0).astype(BF16)
                within_ref[slot, block, :half] = mm(top, value[:half])
                left = mm_t(query[half:], key[:half]).astype(BF16)
                right = jnp.where(keep, mm_t(query[half:], key[half:]), 0.0).astype(BF16)
                within_ref[slot, block, half:] = mm(left, value[:half]) + mm(right, value[half:])


def prefix_kernel(chunk_ref, prior_ref):
    total = jnp.zeros(chunk_ref.shape[1:], F32)
    for chip in range(CHIPS):
        prior_ref[chip] = total.astype(BF16)
        total = total + chunk_ref[chip].astype(F32)


def head_of(y, core, slot):
    if slot == 3:
        return lax.rem(y + 4 * core, DP)
    return lax.rem(y + DP + (slot + 1) * (1 - 2 * core), DP)


def norm_kernel(query_ref, within_ref, prior_ref, s0, s1, s2, s3, gain_ref, own_ref, other_ref):
    core = lax.axis_index("core")
    y = lax.axis_index("dp")
    shares = (core.astype(F32), 1.0 - core.astype(F32))
    for slot, state_ref in enumerate((s0, s1, s2, s3)):
        gain = gain_ref[pl.ds(head_of(y, core, slot), 1), :]
        for block, out_ref in enumerate((own_ref, other_ref)):
            prior = (prior_ref[slot].astype(F32) + shares[block] * state_ref[1 - block]).astype(BF16)
            mixed = within_ref[slot, block] + mm(query_ref[slot, block], prior)
            scale = lax.rsqrt(jnp.mean(mixed * mixed, axis=-1, keepdims=True) + 1e-05)
            out_ref[:, slot * DH : (slot + 1) * DH] = (mixed * scale * gain).astype(BF16)


def out_kernel(own_ref, got_ref, weight_hbm, out_ref, mine, theirs, sems):
    core = lax.axis_index("core")
    y = lax.axis_index("dp")
    copies = []
    for side, (place, buffer) in enumerate(((core, mine), (1 - core, theirs))):
        for slot in range(SLOTS):
            begin = pl.multiple_of(head_of(y, place, slot) * DH, DH)
            copy = pltpu.make_async_copy(
                weight_hbm.at[pl.ds(begin, DH), :], buffer.at[pl.ds(slot * DH, DH), :], sems.at[side * SLOTS + slot]
            )
            copy.start()
            copies.append(copy)
    for copy in copies:
        copy.wait()
    for begin in range(0, D, 256):
        cols = pl.ds(begin, 256)
        out_ref[0, :, cols] = (mm(own_ref[...], mine[:, cols]) + mm(got_ref[...], theirs[:, cols])).astype(BF16)


def body(tokens, w_query, w_key, w_value, w_out, norm_gain):
    own = tokens[0]
    full_out = lax.all_gather(w_out, "dp", axis=0, tiled=True)

    key_1, value_1 = hop(w_key, 1), hop(w_value, 1)
    key_2, value_2 = hop(w_key, 2), hop(w_value, 2)
    other = lax.ppermute(own, "core", SWAP)
    key_3, value_3 = hop(key_2, 1), hop(value_2, 1)
    key_4, value_4 = hop(key_3, 1), hop(value_3, 1)
    w_query, key_1 = lax.optimization_barrier((w_query, key_1))
    query_1, query_2 = hop(w_query, 1), hop(w_query, 2)
    query_3 = hop(query_2, 1)
    query_4 = hop(query_3, 1)

    piece = shape((2, TOK, DH), BF16)
    state = shape((2, DH, DH), F32)
    flops = 2 * 2 * TOK * D * 2 * DH
    one = call(key_value_kernel, (piece, piece, state), flops, 3 << 20, count=4)
    last = call(last_key_value_kernel, (piece, piece, state, shape((SLOTS, DH, DH), BF16)), flops, 3 << 20, count=9)
    k0, v0, s0 = one(own, other, key_1, value_1)
    k1, v1, s1 = one(own, other, key_2, value_2)
    k2, v2, s2 = one(own, other, key_3, value_3)
    k3, v3, s3, total = last(own, other, w_key, w_value, key_4, value_4, s0, s1, s2)

    chunks = total.reshape(CHIPS, SLOTS * DH // CHIPS, DH)
    chunks = lax.all_to_all(chunks, ("z", "x"), 0, 0, tiled=True)
    priors = call(prefix_kernel, shape(chunks.shape, BF16), 1 << 16, 1 << 18, count=1)(chunks)
    prior = lax.all_to_all(priors, ("z", "x"), 0, 0, tiled=True).reshape(SLOTS, DH, DH)

    query, within = call(
        within_kernel,
        (shape((SLOTS, 2, TOK, DH), BF16), shape((SLOTS, 2, TOK, DH), F32)),
        3 * 2 * TOK * D * SLOTS * DH,
        8 << 20,
        count=15,
    )(own, other, query_1, query_2, query_3, w_query, query_4, k0, k1, k2, k3, v0, v1, v2, v3)

    half = shape((TOK, SLOTS * DH), BF16)
    normed_own, normed_other = call(norm_kernel, (half, half), 1 << 28, 4 << 20, count=8)(
        query, within, prior, s0, s1, s2, s3, norm_gain.reshape(DP, DH)
    )
    got = lax.ppermute(normed_other, "core", SWAP)
    weight = pltpu.VMEM((SLOTS * DH, D), BF16)
    return call(
        out_kernel,
        shape((1, TOK, D), BF16),
        1 << 30,
        5 << 20,
        specs=[VMEM, VMEM, HBM],
        scratch=[weight, weight, pltpu.SemaphoreType.DMA((2 * SLOTS,))],
    )(normed_own, got, full_out)


def solution(mesh):
    fine = Mesh(mesh.devices.reshape(DP, ZN, XN, 2), ("dp", "z", "x", "core"))
    seq = ("z", "x", "core")
    in_specs = (
        P("dp", seq, None),
        P(None, "dp"),
        P(None, "dp"),
        P(None, "dp"),
        P("dp", None),
        P(),
    )
    return jax.shard_map(body, mesh=fine, in_specs=in_specs, out_specs=P("dp", seq, None), check_vma=False)
```

```python
import jax
import jax.numpy as jnp
from jax import lax
from jax.experimental import pallas as pl
from jax.experimental.pallas import tpu as pltpu
from jax.sharding import Mesh
from jax.sharding import PartitionSpec as P


DP, ZN, XN = 8, 8, 4
CHIPS = ZN * XN
TOK = 512
D = 1024
DH = 128
HALF = D // 2
SLOTS = 4
F32 = jnp.float32
BF16 = jnp.bfloat16
SWAP = [(0, 1), (1, 0)]
VMEM = pl.BlockSpec(memory_space=pltpu.VMEM)
HBM = pl.BlockSpec(memory_space=pl.ANY)
DMA = pltpu.SemaphoreType.DMA


def toward(distance):
    pairs = []
    for y in range(DP):
        for place in range(2 * CHIPS):
            step = -distance if place % 2 == 0 else distance
            pairs.append((y * 2 * CHIPS + place, (y + step) % DP * 2 * CHIPS + place))
    return pairs


def hop(weight, distance):
    return lax.ppermute(weight, ("dp", "z", "x", "core"), toward(distance))


def call(kernel, count, outs, scratch, flops, moved, spec=HBM, limit=56):
    return pl.pallas_call(
        kernel,
        out_shape=outs,
        in_specs=[spec] * count,
        out_specs=jax.tree.map(lambda _: spec, outs),
        scratch_shapes=scratch,
        compiler_params=pltpu.CompilerParams(vmem_limit_bytes=limit * 1024 * 1024),
        cost_estimate=pl.CostEstimate(flops=flops, bytes_accessed=moved, transcendentals=0),
    )


def shape(dims, kind):
    return jax.ShapeDtypeStruct(dims, kind)


def mm(a, b):
    return jnp.dot(a, b, preferred_element_type=F32)


def mm_t(a, b):
    return lax.dot_general(a, b, (((1,), (1,)), ((), ())), preferred_element_type=F32)


def t_mm(a, b):
    return lax.dot_general(a, b, (((0,), (0,)), ((), ())), preferred_element_type=F32)


def begin(source, target, sem):
    copy = pltpu.make_async_copy(source, target, sem)
    copy.start()
    return copy


def head_of(y, core, slot):
    if slot == 3:
        return lax.rem(y + 4 * core, DP)
    return lax.rem(y + DP + (slot + 1) * (1 - 2 * core), DP)


def pack_kernel(wq, wo, part, sems):
    core = lax.axis_index("core")
    start = pl.multiple_of(core * HALF, HALF)
    copies = [begin(wq.at[pl.ds(start, HALF), :], part.at[pl.ds(0, HALF), :], sems.at[0])]
    for c in range(4):
        cols = pl.ds(pl.multiple_of(core * HALF + c * DH, DH), DH)
        copies.append(begin(wo.at[:, cols], part.at[pl.ds(HALF + c * DH, DH), :], sems.at[1 + c]))
    for copy in copies:
        copy.wait()


def project(own, other, loads, kv, state, tokens, weight, kv_out, state_out, sems):
    copies = [begin(ref, tokens.at[block], sems.at[2 + block]) for block, ref in enumerate((own, other))]
    for load in loads:
        load.wait()
    for block in range(2):
        copies[block].wait()
        both = mm(tokens[block], weight[...]).astype(BF16)
        kv_out[block] = both
        state_out[block] = t_mm(both[:, :DH], both[:, DH:])
    return [begin(kv_out, kv, sems.at[4]), begin(state_out, state, sems.at[5])]


def key_value_kernel(own, other, wk, wv, kv, state, tokens, weight, kv_out, state_out, sems):
    loads = [
        begin(wk, weight.at[:, pl.ds(0, DH)], sems.at[0]),
        begin(wv, weight.at[:, pl.ds(DH, DH)], sems.at[1]),
    ]
    for copy in project(own, other, loads, kv, state, tokens, weight, kv_out, state_out, sems):
        copy.wait()


def last_key_value_kernel(
    own, other, wk, wv, wk_far, wv_far, s0, s1, s2, kv, state, total, tokens, weight, kv_out, state_out, sums, total_out, sems
):
    core = lax.axis_index("core")
    left, right = weight.at[:, pl.ds(0, DH)], weight.at[:, pl.ds(DH, DH)]

    @pl.when(core == 0)
    def _():
        begin(wk, left, sems.at[0])
        begin(wv, right, sems.at[1])

    @pl.when(core != 0)
    def _():
        begin(wk_far, left, sems.at[0])
        begin(wv_far, right, sems.at[1])

    loads = [pltpu.make_async_copy(wk, left, sems.at[0]), pltpu.make_async_copy(wv, right, sems.at[1])]
    early = [begin(ref, sums.at[slot], sems.at[6 + slot]) for slot, ref in enumerate((s0, s1, s2))]
    copies = project(own, other, loads, kv, state, tokens, weight, kv_out, state_out, sems)
    for slot in range(3):
        early[slot].wait()
        total_out[slot] = (sums[slot, 0] + sums[slot, 1]).astype(BF16)
    total_out[3] = (state_out[0] + state_out[1]).astype(BF16)
    copies.append(begin(total_out, total, sems.at[9]))
    for copy in copies:
        copy.wait()


def within_kernel(
    own, other, mine, theirs, kv0, kv1, kv2, kv3, query_ref, within_ref, tokens, weight, kv, query, within, sems, out_sems
):
    core = lax.axis_index("core")
    y = lax.axis_index("dp")
    loads = [begin(ref, tokens.at[block], sems.at[block]) for block, ref in enumerate((own, other))]
    weights, pairs = [], []
    for slot in range(SLOTS):
        head = head_of(y, core, slot)
        cols = pl.ds(slot * DH, DH)
        weights.append([])
        for side, (source, place) in enumerate(((mine, core), (theirs, 1 - core))):
            rows = pl.ds(pl.multiple_of(place * HALF, HALF), HALF)
            sem = sems.at[2 + 2 * slot + side]
            weights[slot].append(begin(source.at[head, pl.ds(0, HALF), :], weight.at[rows, cols], sem))
    for slot, ref in enumerate((kv0, kv1, kv2, kv3)):
        pairs.append(begin(ref, kv.at[slot], sems.at[10 + slot]))
    half = TOK // 2
    rows = lax.broadcasted_iota(jnp.int32, (half, half), 0)
    cols = lax.broadcasted_iota(jnp.int32, (half, half), 1)
    keep = cols <= rows
    for load in loads:
        load.wait()
    copies = []
    for pair in range(2):
        for slot in (2 * pair, 2 * pair + 1):
            for load in weights[slot]:
                load.wait()
            pairs[slot].wait()
        for block in range(2):
            both = mm(tokens[block], weight[:, 2 * pair * DH : 2 * (pair + 1) * DH]).astype(BF16)
            for side in range(2):
                slot = 2 * pair + side
                q = both[:, side * DH : (side + 1) * DH]
                query[slot, block] = q
                copies.append(begin(query.at[slot, block], query_ref.at[slot, block], out_sems.at[0, slot, block]))
                key, value = kv[slot, block, :, :DH], kv[slot, block, :, DH:]
                top = jnp.where(keep, mm_t(q[:half], key[:half]), 0.0).astype(BF16)
                within[slot, block, :half] = mm(top, value[:half])
                left = mm_t(q[half:], key[:half]).astype(BF16)
                right = jnp.where(keep, mm_t(q[half:], key[half:]), 0.0).astype(BF16)
                within[slot, block, half:] = mm(left, value[:half]) + mm(right, value[half:])
                copies.append(begin(within.at[slot, block], within_ref.at[slot, block], out_sems.at[1, slot, block]))
    for copy in copies:
        copy.wait()


def prefix_kernel(chunk_ref, prior_ref):
    total = jnp.zeros(chunk_ref.shape[1:], F32)
    for chip in range(CHIPS):
        prior_ref[chip] = total.astype(BF16)
        total = total + chunk_ref[chip].astype(F32)


def norm_kernel(
    query_ref, within_ref, prior_ref, s0, s1, s2, s3, gain_ref, own_ref, other_ref,
    query, within, prior, state, gain, own, other, sems,
):
    core = lax.axis_index("core")
    y = lax.axis_index("dp")
    first = [begin(prior_ref, prior, sems.at[0]), begin(gain_ref, gain, sems.at[1])]
    loads = []
    for slot, ref in enumerate((s0, s1, s2, s3)):
        loads.append(
            [
                begin(ref, state.at[slot], sems.at[2 + 3 * slot]),
                begin(query_ref.at[slot], query.at[slot], sems.at[3 + 3 * slot]),
                begin(within_ref.at[slot], within.at[slot], sems.at[4 + 3 * slot]),
            ]
        )
    for load in first:
        load.wait()
    shares = (core.astype(F32), 1.0 - core.astype(F32))
    for slot in range(SLOTS):
        for load in loads[slot]:
            load.wait()
        g = gain[pl.ds(head_of(y, core, slot), 1), :]
        for block, out in enumerate((own, other)):
            before = (prior[slot].astype(F32) + shares[block] * state[slot, 1 - block]).astype(BF16)
            mixed = within[slot, block] + mm(query[slot, block], before)
            scale = lax.rsqrt(jnp.mean(mixed * mixed, axis=-1, keepdims=True) + 1e-05)
            out[:, slot * DH : (slot + 1) * DH] = (mixed * scale * g).astype(BF16)
    copies = [begin(own, own_ref, sems.at[14]), begin(other, other_ref, sems.at[15])]
    for copy in copies:
        copy.wait()


def out_kernel(own_ref, got_ref, mine, theirs, out_ref, normed, weight, out, sems, out_sems):
    core = lax.axis_index("core")
    y = lax.axis_index("dp")
    loads = [
        begin(own_ref, normed.at[:, pl.ds(0, HALF)], sems.at[0]),
        begin(got_ref, normed.at[:, pl.ds(HALF, HALF)], sems.at[1]),
    ]
    weights = ([], [])
    for side, (source, where) in enumerate(((mine, core), (theirs, 1 - core))):
        for place in range(2):
            for slot in range(SLOTS):
                head = head_of(y, core if place == 0 else 1 - core, slot)
                index = place * SLOTS + slot
                weights[side].append(
                    begin(source.at[head, pl.ds(HALF, HALF), :], weight.at[side, index], sems.at[2 + side * 8 + index])
                )
    for load in loads:
        load.wait()
    copies = []
    for side, where in enumerate((core, 1 - core)):
        for load in weights[side]:
            load.wait()
        for c in range(0, 4, 2):
            w = jnp.concatenate(
                [
                    jnp.concatenate([weight[side, i, (c + k) * DH : (c + k + 1) * DH, :] for i in range(DP)], axis=0)
                    for k in range(2)
                ],
                axis=1,
            )
            out[side, :, c * DH : (c + 2) * DH] = mm(normed[...], w).astype(BF16)
        cols = pl.ds(pl.multiple_of(where * HALF, HALF), HALF)
        copies.append(begin(out.at[side], out_ref.at[0, :, cols], out_sems.at[side]))
    for copy in copies:
        copy.wait()


def body(tokens, w_query, w_key, w_value, w_out, norm_gain):
    own = tokens[0]
    key_1, value_1 = hop(w_key, 1), hop(w_value, 1)
    other = lax.ppermute(own, "core", SWAP)
    key_2, value_2 = hop(w_key, 2), hop(w_value, 2)

    part = call(pack_kernel, 2, shape((D, DH), BF16), [DMA((5,))], 0, 1 << 19)(w_query, w_out)
    mine = lax.all_gather(part, "dp")

    pair = shape((2, TOK, 2 * DH), BF16)
    state = shape((2, DH, DH), F32)
    flops = 2 * 2 * TOK * D * 2 * DH
    room = [
        pltpu.VMEM((2, TOK, D), BF16),
        pltpu.VMEM((D, 2 * DH), BF16),
        pltpu.VMEM((2, TOK, 2 * DH), BF16),
        pltpu.VMEM((2, DH, DH), F32),
    ]
    one = call(key_value_kernel, 4, (pair, state), [*room, DMA((6,))], flops, 3 << 20, HBM, 16)
    last = call(
        last_key_value_kernel,
        9,
        (pair, state, shape((SLOTS, DH, DH), BF16)),
        [*room, pltpu.VMEM((3, 2, DH, DH), F32), pltpu.VMEM((SLOTS, DH, DH), BF16), DMA((10,))],
        flops,
        3 << 20,
        HBM,
        16,
    )
    kv0, s0 = one(own, other, key_1, value_1)
    key_2, value_2, s0 = lax.optimization_barrier((key_2, value_2, s0))
    key_3, value_3 = hop(key_2, 1), hop(value_2, 1)
    kv1, s1 = one(own, other, key_2, value_2)
    key_3, value_3, s1 = lax.optimization_barrier((key_3, value_3, s1))
    key_4, value_4 = hop(key_3, 1), hop(value_3, 1)
    kv2, s2 = one(own, other, key_3, value_3)
    kv3, s3, total = last(own, other, w_key, w_value, key_4, value_4, s0, s1, s2)

    chunks = total.reshape(CHIPS, SLOTS * DH // CHIPS, DH)
    chunks = lax.all_to_all(chunks, ("z", "x"), 0, 0, tiled=True)
    mine, chunks = lax.optimization_barrier((mine, chunks))
    theirs = lax.ppermute(mine, "core", SWAP)
    priors = call(prefix_kernel, 1, shape(chunks.shape, BF16), [], 1 << 16, 1 << 18, VMEM, 4)(chunks)
    prior = lax.all_to_all(priors, ("z", "x"), 0, 0, tiled=True).reshape(SLOTS, DH, DH)

    queries, withins = (SLOTS, 2, TOK, DH), (SLOTS, 2, TOK, DH)
    query, within = call(
        within_kernel,
        8,
        (shape(queries, BF16), shape(withins, F32)),
        [
            pltpu.VMEM((2, TOK, D), BF16),
            pltpu.VMEM((D, SLOTS * DH), BF16),
            pltpu.VMEM((SLOTS, 2, TOK, 2 * DH), BF16),
            pltpu.VMEM(queries, BF16),
            pltpu.VMEM(withins, F32),
            DMA((14,)),
            DMA((2, SLOTS, 2)),
        ],
        3 * 2 * TOK * D * SLOTS * DH,
        8 << 20,
    )(own, other, mine, theirs, kv0, kv1, kv2, kv3)

    normed = (TOK, SLOTS * DH)
    normed_own, normed_other = call(
        norm_kernel,
        8,
        (shape(normed, BF16), shape(normed, BF16)),
        [
            pltpu.VMEM(queries, BF16),
            pltpu.VMEM(withins, F32),
            pltpu.VMEM((SLOTS, DH, DH), BF16),
            pltpu.VMEM((SLOTS, 2, DH, DH), F32),
            pltpu.VMEM((DP, DH), F32),
            pltpu.VMEM(normed, BF16),
            pltpu.VMEM(normed, BF16),
            DMA((16,)),
        ],
        1 << 28,
        4 << 20,
    )(query, within, prior, s0, s1, s2, s3, norm_gain.reshape(DP, DH))
    got = lax.ppermute(normed_other, "core", SWAP)
    return call(
        out_kernel,
        4,
        shape((1, TOK, D), BF16),
        [
            pltpu.VMEM((TOK, D), BF16),
            pltpu.VMEM((2, DP, HALF, DH), BF16),
            pltpu.VMEM((2, TOK, HALF), BF16),
            DMA((18,)),
            DMA((2,)),
        ],
        1 << 30,
        5 << 20,
    )(normed_own, got, mine, theirs)


def solution(mesh):
    fine = Mesh(mesh.devices.reshape(DP, ZN, XN, 2), ("dp", "z", "x", "core"))
    seq = ("z", "x", "core")
    in_specs = (
        P("dp", seq, None),
        P(None, "dp"),
        P(None, "dp"),
        P(None, "dp"),
        P("dp", None),
        P(),
    )
    return jax.shard_map(body, mesh=fine, in_specs=in_specs, out_specs=P("dp", seq, None), check_vma=False)
```

```python
import jax
import jax.numpy as jnp
from jax import lax
from jax.experimental import pallas as pl
from jax.experimental.pallas import tpu as pltpu
from jax.sharding import Mesh
from jax.sharding import PartitionSpec as P


DP, ZN, XN = 8, 8, 4
CHIPS = ZN * XN
TOK = 512
D = 1024
DH = 128
HALF = D // 2
SLOTS = 4
F32 = jnp.float32
BF16 = jnp.bfloat16
SWAP = [(0, 1), (1, 0)]
VMEM = pl.BlockSpec(memory_space=pltpu.VMEM)
HBM = pl.BlockSpec(memory_space=pl.ANY)
DMA = pltpu.SemaphoreType.DMA


def hop(weight):
    pairs = []
    for y in range(DP):
        for place in range(2 * CHIPS):
            step = -1 if place % 2 == 0 else 1
            pairs.append((y * 2 * CHIPS + place, (y + step) % DP * 2 * CHIPS + place))
    return lax.ppermute(weight, ("dp", "z", "x", "core"), pairs)


def call(kernel, count, outs, scratch, flops, moved, spec=HBM, limit=56):
    return pl.pallas_call(
        kernel,
        out_shape=outs,
        in_specs=[spec] * count,
        out_specs=jax.tree.map(lambda _: spec, outs),
        scratch_shapes=scratch,
        compiler_params=pltpu.CompilerParams(vmem_limit_bytes=limit * 1024 * 1024),
        cost_estimate=pl.CostEstimate(flops=flops, bytes_accessed=moved, transcendentals=0),
    )


def shape(dims, kind):
    return jax.ShapeDtypeStruct(dims, kind)


def mm(a, b):
    return jnp.dot(a, b, preferred_element_type=F32)


def mm_t(a, b):
    return lax.dot_general(a, b, (((1,), (1,)), ((), ())), preferred_element_type=F32)


def t_mm(a, b):
    return lax.dot_general(a, b, (((0,), (0,)), ((), ())), preferred_element_type=F32)


def begin(source, target, sem):
    copy = pltpu.make_async_copy(source, target, sem)
    copy.start()
    return copy


def head_of(y, core, slot):
    if slot == 3:
        return lax.rem(y + 4 * core, DP)
    return lax.rem(y + DP + (slot + 1) * (1 - 2 * core), DP)


def project(own, other, loads, kv, state, tokens, weight, kv_out, state_out, sems):
    copies = [begin(ref, tokens.at[block], sems.at[2 + block]) for block, ref in enumerate((own, other))]
    for load in loads:
        load.wait()
    for block in range(2):
        copies[block].wait()
        both = mm(tokens[block], weight[...]).astype(BF16)
        kv_out[block] = both
        state_out[block] = t_mm(both[:, :DH], both[:, DH:])
    return [begin(kv_out, kv, sems.at[4]), begin(state_out, state, sems.at[5])]


def key_value_kernel(own, other, wk, wv, kv, state, tokens, weight, kv_out, state_out, sems):
    loads = [
        begin(wk, weight.at[:, pl.ds(0, DH)], sems.at[0]),
        begin(wv, weight.at[:, pl.ds(DH, DH)], sems.at[1]),
    ]
    for copy in project(own, other, loads, kv, state, tokens, weight, kv_out, state_out, sems):
        copy.wait()


def last_key_value_kernel(
    own, other, wk, wv, wk_far, wv_far, s0, s1, s2, kv, state, total, tokens, weight, kv_out, state_out, sums, total_out, sems
):
    core = lax.axis_index("core")
    left, right = weight.at[:, pl.ds(0, DH)], weight.at[:, pl.ds(DH, DH)]

    @pl.when(core == 0)
    def _():
        begin(wk, left, sems.at[0])
        begin(wv, right, sems.at[1])

    @pl.when(core != 0)
    def _():
        begin(wk_far, left, sems.at[0])
        begin(wv_far, right, sems.at[1])

    loads = [pltpu.make_async_copy(wk, left, sems.at[0]), pltpu.make_async_copy(wv, right, sems.at[1])]
    early = [begin(ref, sums.at[slot], sems.at[6 + slot]) for slot, ref in enumerate((s0, s1, s2))]
    copies = project(own, other, loads, kv, state, tokens, weight, kv_out, state_out, sems)
    for slot in range(3):
        early[slot].wait()
        total_out[slot] = (sums[slot, 0] + sums[slot, 1]).astype(BF16)
    total_out[3] = (state_out[0] + state_out[1]).astype(BF16)
    copies.append(begin(total_out, total, sems.at[9]))
    for copy in copies:
        copy.wait()


def within_kernel(
    own, other, q0, q1, q2, q_own, q_far, kv0, kv1, kv2, kv3, query_ref, within_ref,
    tokens, weight, kv, query, within, sems, out_sems,
):
    core = lax.axis_index("core")
    loads = [begin(ref, tokens.at[block], sems.at[block]) for block, ref in enumerate((own, other))]
    weights, pairs = [], []
    for slot, ref in enumerate((q0, q1, q2)):
        weights.append(begin(ref, weight.at[:, pl.ds(slot * DH, DH)], sems.at[2 + slot]))
    final = weight.at[:, pl.ds(3 * DH, DH)]

    @pl.when(core == 0)
    def _():
        begin(q_own, final, sems.at[5])

    @pl.when(core != 0)
    def _():
        begin(q_far, final, sems.at[5])

    weights.append(pltpu.make_async_copy(q_own, final, sems.at[5]))
    for slot, ref in enumerate((kv0, kv1, kv2, kv3)):
        pairs.append(begin(ref, kv.at[slot], sems.at[10 + slot]))
    half = TOK // 2
    rows = lax.broadcasted_iota(jnp.int32, (half, half), 0)
    cols = lax.broadcasted_iota(jnp.int32, (half, half), 1)
    keep = cols <= rows
    for load in loads:
        load.wait()
    copies = []
    for pair in range(2):
        for slot in (2 * pair, 2 * pair + 1):
            weights[slot].wait()
            pairs[slot].wait()
        for block in range(2):
            both = mm(tokens[block], weight[:, 2 * pair * DH : 2 * (pair + 1) * DH]).astype(BF16)
            for side in range(2):
                slot = 2 * pair + side
                q = both[:, side * DH : (side + 1) * DH]
                query[slot, block] = q
                copies.append(begin(query.at[slot, block], query_ref.at[slot, block], out_sems.at[0, slot, block]))
                key, value = kv[slot, block, :, :DH], kv[slot, block, :, DH:]
                top = jnp.where(keep, mm_t(q[:half], key[:half]), 0.0).astype(BF16)
                within[slot, block, :half] = mm(top, value[:half])
                left = mm_t(q[half:], key[:half]).astype(BF16)
                right = jnp.where(keep, mm_t(q[half:], key[half:]), 0.0).astype(BF16)
                within[slot, block, half:] = mm(left, value[:half]) + mm(right, value[half:])
                copies.append(begin(within.at[slot, block], within_ref.at[slot, block], out_sems.at[1, slot, block]))
    for copy in copies:
        copy.wait()


def prefix_kernel(chunk_ref, prior_ref):
    total = jnp.zeros(chunk_ref.shape[1:], F32)
    for chip in range(CHIPS):
        prior_ref[chip] = total.astype(BF16)
        total = total + chunk_ref[chip].astype(F32)


def norm_kernel(
    query_ref, within_ref, prior_ref, s0, s1, s2, s3, gain_ref, own_ref, other_ref,
    query, within, prior, state, gain, own, other, sems,
):
    core = lax.axis_index("core")
    y = lax.axis_index("dp")
    first = [begin(prior_ref, prior, sems.at[0]), begin(gain_ref, gain, sems.at[1])]
    loads = []
    for slot, ref in enumerate((s0, s1, s2, s3)):
        loads.append(
            [
                begin(ref, state.at[slot], sems.at[2 + 3 * slot]),
                begin(query_ref.at[slot], query.at[slot], sems.at[3 + 3 * slot]),
                begin(within_ref.at[slot], within.at[slot], sems.at[4 + 3 * slot]),
            ]
        )
    for load in first:
        load.wait()
    shares = (core.astype(F32), 1.0 - core.astype(F32))
    for slot in range(SLOTS):
        for load in loads[slot]:
            load.wait()
        g = gain[pl.ds(head_of(y, core, slot), 1), :]
        for block, out in enumerate((own, other)):
            before = (prior[slot].astype(F32) + shares[block] * state[slot, 1 - block]).astype(BF16)
            mixed = within[slot, block] + mm(query[slot, block], before)
            scale = lax.rsqrt(jnp.mean(mixed * mixed, axis=-1, keepdims=True) + 1e-05)
            out[:, slot * DH : (slot + 1) * DH] = (mixed * scale * g).astype(BF16)
    copies = [begin(own, own_ref, sems.at[14]), begin(other, other_ref, sems.at[15])]
    for copy in copies:
        copy.wait()


def out_kernel(own_ref, got_ref, weight_ref, out_ref, normed, weight, out, sems, out_sems):
    core = lax.axis_index("core")
    y = lax.axis_index("dp")
    loads = [
        begin(own_ref, normed.at[:, pl.ds(0, HALF)], sems.at[0]),
        begin(got_ref, normed.at[:, pl.ds(HALF, HALF)], sems.at[1]),
    ]
    for place in range(2):
        for slot in range(SLOTS):
            rows = pl.ds(pl.multiple_of(head_of(y, core if place == 0 else 1 - core, slot) * DH, DH), DH)
            index = place * SLOTS + slot
            loads.append(begin(weight_ref.at[rows, :], weight.at[pl.ds(index * DH, DH), :], sems.at[2 + index]))
    for load in loads:
        load.wait()
    copies = []
    for c in range(4):
        cols = pl.ds(c * 2 * DH, 2 * DH)
        out[:, cols] = mm(normed[...], weight[:, cols]).astype(BF16)
        copies.append(begin(out.at[:, cols], out_ref.at[0, :, cols], out_sems.at[c]))
    for copy in copies:
        copy.wait()


def body(tokens, w_query, w_key, w_value, w_out, norm_gain):
    own = tokens[0]
    key_1, value_1, query_1 = hop(w_key), hop(w_value), hop(w_query)
    other = lax.ppermute(own, "core", SWAP)

    pair = shape((2, TOK, 2 * DH), BF16)
    state = shape((2, DH, DH), F32)
    flops = 2 * 2 * TOK * D * 2 * DH
    room = [
        pltpu.VMEM((2, TOK, D), BF16),
        pltpu.VMEM((D, 2 * DH), BF16),
        pltpu.VMEM((2, TOK, 2 * DH), BF16),
        pltpu.VMEM((2, DH, DH), F32),
    ]
    one = call(key_value_kernel, 4, (pair, state), [*room, DMA((6,))], flops, 3 << 20, HBM, 16)
    last = call(
        last_key_value_kernel,
        9,
        (pair, state, shape((SLOTS, DH, DH), BF16)),
        [*room, pltpu.VMEM((3, 2, DH, DH), F32), pltpu.VMEM((SLOTS, DH, DH), BF16), DMA((10,))],
        flops,
        3 << 20,
        HBM,
        16,
    )
    kv0, s0 = one(own, other, key_1, value_1)
    key_2, value_2, query_2 = hop(key_1), hop(value_1), hop(query_1)
    key_2, value_2, s0 = lax.optimization_barrier((key_2, value_2, s0))
    kv1, s1 = one(own, other, key_2, value_2)
    w_out, key_2 = lax.optimization_barrier((w_out, key_2))
    full_out = lax.all_gather(w_out, "dp", axis=0, tiled=True)
    key_3, value_3, query_3 = hop(key_2), hop(value_2), hop(query_2)
    key_3, value_3, s1 = lax.optimization_barrier((key_3, value_3, s1))
    kv2, s2 = one(own, other, key_3, value_3)
    key_4, value_4, query_4 = hop(key_3), hop(value_3), hop(query_3)
    kv3, s3, total = last(own, other, w_key, w_value, key_4, value_4, s0, s1, s2)

    chunks = total.reshape(CHIPS, SLOTS * DH // CHIPS, DH)
    chunks = lax.all_to_all(chunks, ("z", "x"), 0, 0, tiled=True)
    priors = call(prefix_kernel, 1, shape(chunks.shape, BF16), [], 1 << 16, 1 << 18, VMEM, 4)(chunks)
    prior = lax.all_to_all(priors, ("z", "x"), 0, 0, tiled=True).reshape(SLOTS, DH, DH)

    queries, withins = (SLOTS, 2, TOK, DH), (SLOTS, 2, TOK, DH)
    query, within = call(
        within_kernel,
        11,
        (shape(queries, BF16), shape(withins, F32)),
        [
            pltpu.VMEM((2, TOK, D), BF16),
            pltpu.VMEM((D, SLOTS * DH), BF16),
            pltpu.VMEM((SLOTS, 2, TOK, 2 * DH), BF16),
            pltpu.VMEM(queries, BF16),
            pltpu.VMEM(withins, F32),
            DMA((14,)),
            DMA((2, SLOTS, 2)),
        ],
        3 * 2 * TOK * D * SLOTS * DH,
        8 << 20,
    )(own, other, query_1, query_2, query_3, w_query, query_4, kv0, kv1, kv2, kv3)

    normed = (TOK, SLOTS * DH)
    normed_own, normed_other = call(
        norm_kernel,
        8,
        (shape(normed, BF16), shape(normed, BF16)),
        [
            pltpu.VMEM(queries, BF16),
            pltpu.VMEM(withins, F32),
            pltpu.VMEM((SLOTS, DH, DH), BF16),
            pltpu.VMEM((SLOTS, 2, DH, DH), F32),
            pltpu.VMEM((DP, DH), F32),
            pltpu.VMEM(normed, BF16),
            pltpu.VMEM(normed, BF16),
            DMA((16,)),
        ],
        1 << 28,
        4 << 20,
    )(query, within, prior, s0, s1, s2, s3, norm_gain.reshape(DP, DH))
    got = lax.ppermute(normed_other, "core", SWAP)
    return call(
        out_kernel,
        3,
        shape((1, TOK, D), BF16),
        [
            pltpu.VMEM((TOK, D), BF16),
            pltpu.VMEM((D, D), BF16),
            pltpu.VMEM((TOK, D), BF16),
            DMA((10,)),
            DMA((4,)),
        ],
        1 << 30,
        5 << 20,
    )(normed_own, got, full_out)


def solution(mesh):
    fine = Mesh(mesh.devices.reshape(DP, ZN, XN, 2), ("dp", "z", "x", "core"))
    seq = ("z", "x", "core")
    in_specs = (
        P("dp", seq, None),
        P(None, "dp"),
        P(None, "dp"),
        P(None, "dp"),
        P("dp", None),
        P(),
    )
    return jax.shard_map(body, mesh=fine, in_specs=in_specs, out_specs=P("dp", seq, None), check_vma=False)
```

```python
import functools

import jax
import jax.numpy as jnp
from jax import lax
from jax.experimental import pallas as pl
from jax.experimental.pallas import tpu as pltpu
from jax.sharding import Mesh
from jax.sharding import PartitionSpec as P


DP, ZN, XN = 8, 8, 4
CHIPS = ZN * XN
TOK = 512
D = 1024
DH = 128
HALF = D // 2
SLOTS = 4
F32 = jnp.float32
BF16 = jnp.bfloat16
SWAP = [(0, 1), (1, 0)]
VMEM = pl.BlockSpec(memory_space=pltpu.VMEM)
HBM = pl.BlockSpec(memory_space=pl.ANY)
DMA = pltpu.SemaphoreType.DMA


def hop(weight):
    pairs = []
    for y in range(DP):
        for place in range(2 * CHIPS):
            step = -1 if place % 2 == 0 else 1
            pairs.append((y * 2 * CHIPS + place, (y + step) % DP * 2 * CHIPS + place))
    return lax.ppermute(weight, ("dp", "z", "x", "core"), pairs)


def call(kernel, count, outs, scratch, flops, moved, spec=HBM, limit=56):
    return pl.pallas_call(
        kernel,
        out_shape=outs,
        in_specs=[spec] * count,
        out_specs=jax.tree.map(lambda _: spec, outs),
        scratch_shapes=scratch,
        compiler_params=pltpu.CompilerParams(vmem_limit_bytes=limit * 1024 * 1024),
        cost_estimate=pl.CostEstimate(flops=flops, bytes_accessed=moved, transcendentals=0),
    )


def shape(dims, kind):
    return jax.ShapeDtypeStruct(dims, kind)


def mm(a, b):
    return jnp.dot(a, b, preferred_element_type=F32)


def mm_t(a, b):
    return lax.dot_general(a, b, (((1,), (1,)), ((), ())), preferred_element_type=F32)


def t_mm(a, b):
    return lax.dot_general(a, b, (((0,), (0,)), ((), ())), preferred_element_type=F32)


def begin(source, target, sem):
    copy = pltpu.make_async_copy(source, target, sem)
    copy.start()
    return copy


def head_of(y, core, slot):
    if slot == 3:
        return lax.rem(y + 4 * core, DP)
    return lax.rem(y + DP + (slot + 1) * (1 - 2 * core), DP)


def project(own, other, loads, kv, state, tokens, weight, kv_out, state_out, sems):
    copies = [begin(ref, tokens.at[block], sems.at[2 + block]) for block, ref in enumerate((own, other))]
    for load in loads:
        load.wait()
    for block in range(2):
        copies[block].wait()
        both = mm(tokens[block], weight[...]).astype(BF16)
        kv_out[block] = both
        state_out[block] = t_mm(both[:, :DH], both[:, DH:])
    return [begin(kv_out, kv, sems.at[4]), begin(state_out, state, sems.at[5])]


def key_value_kernel(own, other, wk, wv, kv, state, tokens, weight, kv_out, state_out, sems):
    loads = [
        begin(wk, weight.at[:, pl.ds(0, DH)], sems.at[0]),
        begin(wv, weight.at[:, pl.ds(DH, DH)], sems.at[1]),
    ]
    for copy in project(own, other, loads, kv, state, tokens, weight, kv_out, state_out, sems):
        copy.wait()


def last_key_value_kernel(
    own, other, wk, wv, wk_far, wv_far, s0, s1, s2, kv, state, total, tokens, weight, kv_out, state_out, sums, total_out, sems
):
    core = lax.axis_index("core")
    left, right = weight.at[:, pl.ds(0, DH)], weight.at[:, pl.ds(DH, DH)]

    @pl.when(core == 0)
    def _():
        begin(wk, left, sems.at[0])
        begin(wv, right, sems.at[1])

    @pl.when(core != 0)
    def _():
        begin(wk_far, left, sems.at[0])
        begin(wv_far, right, sems.at[1])

    loads = [pltpu.make_async_copy(wk, left, sems.at[0]), pltpu.make_async_copy(wv, right, sems.at[1])]
    early = [begin(ref, sums.at[slot], sems.at[6 + slot]) for slot, ref in enumerate((s0, s1, s2))]
    copies = project(own, other, loads, kv, state, tokens, weight, kv_out, state_out, sems)
    for slot in range(3):
        early[slot].wait()
        total_out[slot] = (sums[slot, 0] + sums[slot, 1]).astype(BF16)
    total_out[3] = (state_out[0] + state_out[1]).astype(BF16)
    copies.append(begin(total_out, total, sems.at[9]))
    for copy in copies:
        copy.wait()


def within_kernel(
    own, other, q0, q1, q2, q_own, q_far, kv0, kv1, kv2, kv3, query_ref, within_ref,
    tokens, weight, kv, query, within, sems, out_sems,
):
    core = lax.axis_index("core")
    loads = [begin(ref, tokens.at[block], sems.at[block]) for block, ref in enumerate((own, other))]
    weights, pairs = [], []
    for slot, ref in enumerate((q0, q1, q2)):
        weights.append(begin(ref, weight.at[:, pl.ds(slot * DH, DH)], sems.at[2 + slot]))
    final = weight.at[:, pl.ds(3 * DH, DH)]

    @pl.when(core == 0)
    def _():
        begin(q_own, final, sems.at[5])

    @pl.when(core != 0)
    def _():
        begin(q_far, final, sems.at[5])

    weights.append(pltpu.make_async_copy(q_own, final, sems.at[5]))
    for slot, ref in enumerate((kv0, kv1, kv2, kv3)):
        pairs.append(begin(ref, kv.at[slot], sems.at[10 + slot]))
    half = TOK // 2
    rows = lax.broadcasted_iota(jnp.int32, (half, half), 0)
    cols = lax.broadcasted_iota(jnp.int32, (half, half), 1)
    keep = cols <= rows
    for load in loads:
        load.wait()
    copies = []
    for pair in range(2):
        for slot in (2 * pair, 2 * pair + 1):
            weights[slot].wait()
            pairs[slot].wait()
        for block in range(2):
            both = mm(tokens[block], weight[:, 2 * pair * DH : 2 * (pair + 1) * DH]).astype(BF16)
            for side in range(2):
                slot = 2 * pair + side
                q = both[:, side * DH : (side + 1) * DH]
                query[slot, block] = q
                copies.append(begin(query.at[slot, block], query_ref.at[slot, block], out_sems.at[0, slot, block]))
                key, value = kv[slot, block, :, :DH], kv[slot, block, :, DH:]
                top = jnp.where(keep, mm_t(q[:half], key[:half]), 0.0).astype(BF16)
                within[slot, block, :half] = mm(top, value[:half])
                left = mm_t(q[half:], key[:half]).astype(BF16)
                right = jnp.where(keep, mm_t(q[half:], key[half:]), 0.0).astype(BF16)
                within[slot, block, half:] = mm(left, value[:half]) + mm(right, value[half:])
                copies.append(begin(within.at[slot, block], within_ref.at[slot, block], out_sems.at[1, slot, block]))
    for copy in copies:
        copy.wait()


def prefix_kernel(chunk_ref, prior_ref):
    total = jnp.zeros(chunk_ref.shape[1:], F32)
    for chip in range(CHIPS):
        prior_ref[chip] = total.astype(BF16)
        total = total + chunk_ref[chip].astype(F32)


def out_kernel(
    block, query_ref, within_ref, prior_ref, s0, s1, s2, s3, gain_ref, o0, o1, o2, o_own, o_far, out_ref,
    query, within, prior, state, gain, weight, normed, out, sems, out_sems,
):
    core = lax.axis_index("core")
    y = lax.axis_index("dp")
    first = [begin(prior_ref, prior, sems.at[0]), begin(gain_ref, gain, sems.at[1])]
    loads, weights = [], []
    for slot, ref in enumerate((s0, s1, s2, s3)):
        loads.append(
            [
                begin(ref.at[1 - block], state.at[slot], sems.at[2 + 3 * slot]),
                begin(query_ref.at[slot, block], query.at[slot], sems.at[3 + 3 * slot]),
                begin(within_ref.at[slot, block], within.at[slot], sems.at[4 + 3 * slot]),
            ]
        )
    for slot, ref in enumerate((o0, o1, o2)):
        weights.append(begin(ref, weight.at[pl.ds(slot * DH, DH), :], sems.at[14 + slot]))
    final = weight.at[pl.ds(3 * DH, DH), :]

    @pl.when(core == 0)
    def _():
        begin(o_own, final, sems.at[17])

    @pl.when(core != 0)
    def _():
        begin(o_far, final, sems.at[17])

    weights.append(pltpu.make_async_copy(o_own, final, sems.at[17]))
    for load in first:
        load.wait()
    share = (core if block == 0 else 1 - core).astype(F32)
    for slot in range(SLOTS):
        for load in loads[slot]:
            load.wait()
        g = gain[pl.ds(head_of(y, core, slot), 1), :]
        before = (prior[slot].astype(F32) + share * state[slot]).astype(BF16)
        mixed = within[slot] + mm(query[slot], before)
        scale = lax.rsqrt(jnp.mean(mixed * mixed, axis=-1, keepdims=True) + 1e-05)
        normed[:, slot * DH : (slot + 1) * DH] = (mixed * scale * g).astype(BF16)
    for load in weights:
        load.wait()
    copies = []
    for c in range(4):
        cols = pl.ds(c * 2 * DH, 2 * DH)
        out[:, cols] = mm(normed[...], weight[:, cols]).astype(out.dtype)
        copies.append(begin(out.at[:, cols], out_ref.at[:, cols], out_sems.at[c]))
    for copy in copies:
        copy.wait()


def body(tokens, w_query, w_key, w_value, w_out, norm_gain):
    own = tokens[0]
    key_1, value_1, query_1 = hop(w_key), hop(w_value), hop(w_query)
    other = lax.ppermute(own, "core", SWAP)

    pair = shape((2, TOK, 2 * DH), BF16)
    state = shape((2, DH, DH), F32)
    flops = 2 * 2 * TOK * D * 2 * DH
    room = [
        pltpu.VMEM((2, TOK, D), BF16),
        pltpu.VMEM((D, 2 * DH), BF16),
        pltpu.VMEM((2, TOK, 2 * DH), BF16),
        pltpu.VMEM((2, DH, DH), F32),
    ]
    one = call(key_value_kernel, 4, (pair, state), [*room, DMA((6,))], flops, 3 << 20, HBM, 16)
    last = call(
        last_key_value_kernel,
        9,
        (pair, state, shape((SLOTS, DH, DH), BF16)),
        [*room, pltpu.VMEM((3, 2, DH, DH), F32), pltpu.VMEM((SLOTS, DH, DH), BF16), DMA((10,))],
        flops,
        3 << 20,
        HBM,
        16,
    )
    kv0, s0 = one(own, other, key_1, value_1)
    key_2, value_2, query_2 = hop(key_1), hop(value_1), hop(query_1)
    key_2, value_2, s0 = lax.optimization_barrier((key_2, value_2, s0))
    kv1, s1 = one(own, other, key_2, value_2)
    key_3, value_3, query_3 = hop(key_2), hop(value_2), hop(query_2)
    key_3, value_3, s1 = lax.optimization_barrier((key_3, value_3, s1))
    kv2, s2 = one(own, other, key_3, value_3)
    key_4, value_4, query_4 = hop(key_3), hop(value_3), hop(query_3)
    w_out, s2 = lax.optimization_barrier((w_out, s2))
    out_1 = hop(w_out)
    out_2 = hop(out_1)
    out_3 = hop(out_2)
    out_4 = hop(out_3)
    kv3, s3, total = last(own, other, w_key, w_value, key_4, value_4, s0, s1, s2)

    chunks = total.reshape(CHIPS, SLOTS * DH // CHIPS, DH)
    chunks = lax.all_to_all(chunks, ("z", "x"), 0, 0, tiled=True)
    priors = call(prefix_kernel, 1, shape(chunks.shape, BF16), [], 1 << 16, 1 << 18, VMEM, 4)(chunks)
    prior = lax.all_to_all(priors, ("z", "x"), 0, 0, tiled=True).reshape(SLOTS, DH, DH)

    queries, withins = (SLOTS, 2, TOK, DH), (SLOTS, 2, TOK, DH)
    query, within = call(
        within_kernel,
        11,
        (shape(queries, BF16), shape(withins, F32)),
        [
            pltpu.VMEM((2, TOK, D), BF16),
            pltpu.VMEM((D, SLOTS * DH), BF16),
            pltpu.VMEM((SLOTS, 2, TOK, 2 * DH), BF16),
            pltpu.VMEM(queries, BF16),
            pltpu.VMEM(withins, F32),
            DMA((14,)),
            DMA((2, SLOTS, 2)),
        ],
        3 * 2 * TOK * D * SLOTS * DH,
        8 << 20,
    )(own, other, query_1, query_2, query_3, w_query, query_4, kv0, kv1, kv2, kv3)

    operands = (query, within, prior, s0, s1, s2, s3, norm_gain.reshape(DP, DH), out_1, out_2, out_3, w_out, out_4)
    partial = []
    for block, kind in ((1, BF16), (0, F32)):
        partial.append(
            call(
                functools.partial(out_kernel, block),
                13,
                shape((TOK, D), kind),
                [
                    pltpu.VMEM((SLOTS, TOK, DH), BF16),
                    pltpu.VMEM((SLOTS, TOK, DH), F32),
                    pltpu.VMEM((SLOTS, DH, DH), BF16),
                    pltpu.VMEM((SLOTS, DH, DH), F32),
                    pltpu.VMEM((DP, DH), F32),
                    pltpu.VMEM((SLOTS * DH, D), BF16),
                    pltpu.VMEM((TOK, SLOTS * DH), BF16),
                    pltpu.VMEM((TOK, D), kind),
                    DMA((18,)),
                    DMA((4,)),
                ],
                5 << 28,
                5 << 20,
                HBM,
                16,
            )(*operands)
        )
    got = lax.ppermute(partial[0], "core", SWAP)
    return (partial[1] + got.astype(F32)).astype(BF16)[None]


def solution(mesh):
    fine = Mesh(mesh.devices.reshape(DP, ZN, XN, 2), ("dp", "z", "x", "core"))
    seq = ("z", "x", "core")
    in_specs = (
        P("dp", seq, None),
        P(None, "dp"),
        P(None, "dp"),
        P(None, "dp"),
        P("dp", None),
        P(),
    )
    return jax.shard_map(body, mesh=fine, in_specs=in_specs, out_specs=P("dp", seq, None), check_vma=False)
```

```python
import functools

import jax
import jax.numpy as jnp
from jax import lax
from jax.experimental import pallas as pl
from jax.experimental.pallas import tpu as pltpu
from jax.sharding import Mesh
from jax.sharding import PartitionSpec as P


DP, ZN, XN = 8, 8, 4
CHIPS = ZN * XN
TOK = 512
D = 1024
DH = 128
HALF = D // 2
SLOTS = 4
F32 = jnp.float32
BF16 = jnp.bfloat16
SWAP = [(0, 1), (1, 0)]
VMEM = pl.BlockSpec(memory_space=pltpu.VMEM)
HBM = pl.BlockSpec(memory_space=pl.ANY)
DMA = pltpu.SemaphoreType.DMA


def hop(weight):
    pairs = []
    for y in range(DP):
        for place in range(2 * CHIPS):
            step = -1 if place % 2 == 0 else 1
            pairs.append((y * 2 * CHIPS + place, (y + step) % DP * 2 * CHIPS + place))
    return lax.ppermute(weight, ("dp", "z", "x", "core"), pairs)


def call(kernel, count, outs, scratch, flops, moved, spec=HBM, limit=56):
    return pl.pallas_call(
        kernel,
        out_shape=outs,
        in_specs=[spec] * count,
        out_specs=jax.tree.map(lambda _: spec, outs),
        scratch_shapes=scratch,
        compiler_params=pltpu.CompilerParams(vmem_limit_bytes=limit * 1024 * 1024),
        cost_estimate=pl.CostEstimate(flops=flops, bytes_accessed=moved, transcendentals=0),
    )


def shape(dims, kind):
    return jax.ShapeDtypeStruct(dims, kind)


def mm(a, b):
    return jnp.dot(a, b, preferred_element_type=F32)


def mm_t(a, b):
    return lax.dot_general(a, b, (((1,), (1,)), ((), ())), preferred_element_type=F32)


def t_mm(a, b):
    return lax.dot_general(a, b, (((0,), (0,)), ((), ())), preferred_element_type=F32)


def begin(source, target, sem):
    copy = pltpu.make_async_copy(source, target, sem)
    copy.start()
    return copy


def head_of(y, core, slot):
    if slot == 3:
        return lax.rem(y + 4 * core, DP)
    return lax.rem(y + DP + (slot + 1) * (1 - 2 * core), DP)


def project(own, other, loads, kv, state, tokens, weight, kv_out, state_out, sems):
    copies = [begin(ref, tokens.at[block], sems.at[2 + block]) for block, ref in enumerate((own, other))]
    for load in loads:
        load.wait()
    for block in range(2):
        copies[block].wait()
        both = mm(tokens[block], weight[...]).astype(BF16)
        kv_out[block] = both
        state_out[block] = t_mm(both[:, :DH], both[:, DH:])
    return [begin(kv_out, kv, sems.at[4]), begin(state_out, state, sems.at[5])]


def key_value_kernel(own, other, wk, wv, kv, state, tokens, weight, kv_out, state_out, sems):
    loads = [
        begin(wk, weight.at[:, pl.ds(0, DH)], sems.at[0]),
        begin(wv, weight.at[:, pl.ds(DH, DH)], sems.at[1]),
    ]
    for copy in project(own, other, loads, kv, state, tokens, weight, kv_out, state_out, sems):
        copy.wait()


def last_key_value_kernel(
    own, other, wk, wv, wk_far, wv_far, s0, s1, s2, kv, state, total, tokens, weight, kv_out, state_out, sums, total_out, sems
):
    core = lax.axis_index("core")
    left, right = weight.at[:, pl.ds(0, DH)], weight.at[:, pl.ds(DH, DH)]

    @pl.when(core == 0)
    def _():
        begin(wk, left, sems.at[0])
        begin(wv, right, sems.at[1])

    @pl.when(core != 0)
    def _():
        begin(wk_far, left, sems.at[0])
        begin(wv_far, right, sems.at[1])

    loads = [pltpu.make_async_copy(wk, left, sems.at[0]), pltpu.make_async_copy(wv, right, sems.at[1])]
    early = [begin(ref, sums.at[slot], sems.at[6 + slot]) for slot, ref in enumerate((s0, s1, s2))]
    copies = project(own, other, loads, kv, state, tokens, weight, kv_out, state_out, sems)
    for slot in range(3):
        early[slot].wait()
        total_out[slot] = (sums[slot, 0] + sums[slot, 1]).astype(BF16)
    total_out[3] = (state_out[0] + state_out[1]).astype(BF16)
    copies.append(begin(total_out, total, sems.at[9]))
    for copy in copies:
        copy.wait()


def within_kernel(
    own, other, q0, q1, q2, q_own, q_far, kv0, kv1, kv2, kv3, query_ref, within_ref,
    tokens, weight, kv, query, within, sems, out_sems,
):
    core = lax.axis_index("core")
    loads = [begin(ref, tokens.at[block], sems.at[block]) for block, ref in enumerate((own, other))]
    weights, pairs = [], []
    for slot, ref in enumerate((q0, q1, q2)):
        weights.append(begin(ref, weight.at[:, pl.ds(slot * DH, DH)], sems.at[2 + slot]))
    final = weight.at[:, pl.ds(3 * DH, DH)]

    @pl.when(core == 0)
    def _():
        begin(q_own, final, sems.at[5])

    @pl.when(core != 0)
    def _():
        begin(q_far, final, sems.at[5])

    weights.append(pltpu.make_async_copy(q_own, final, sems.at[5]))
    for slot, ref in enumerate((kv0, kv1, kv2, kv3)):
        pairs.append(begin(ref, kv.at[slot], sems.at[10 + slot]))
    half = TOK // 2
    rows = lax.broadcasted_iota(jnp.int32, (half, half), 0)
    cols = lax.broadcasted_iota(jnp.int32, (half, half), 1)
    keep = cols <= rows
    for load in loads:
        load.wait()
    copies = []
    for pair in range(2):
        for slot in (2 * pair, 2 * pair + 1):
            weights[slot].wait()
            pairs[slot].wait()
        for block in range(2):
            both = mm(tokens[block], weight[:, 2 * pair * DH : 2 * (pair + 1) * DH]).astype(BF16)
            for side in range(2):
                slot = 2 * pair + side
                q = both[:, side * DH : (side + 1) * DH]
                query[slot, block] = q
                copies.append(begin(query.at[slot, block], query_ref.at[slot, block], out_sems.at[0, slot, block]))
                key, value = kv[slot, block, :, :DH], kv[slot, block, :, DH:]
                top = jnp.where(keep, mm_t(q[:half], key[:half]), 0.0).astype(BF16)
                within[slot, block, :half] = mm(top, value[:half])
                left = mm_t(q[half:], key[:half]).astype(BF16)
                right = jnp.where(keep, mm_t(q[half:], key[half:]), 0.0).astype(BF16)
                within[slot, block, half:] = mm(left, value[:half]) + mm(right, value[half:])
                copies.append(begin(within.at[slot, block], within_ref.at[slot, block], out_sems.at[1, slot, block]))
    for copy in copies:
        copy.wait()


def prefix_kernel(chunk_ref, prior_ref):
    total = jnp.zeros(chunk_ref.shape[1:], F32)
    for chip in range(CHIPS):
        prior_ref[chip] = total.astype(BF16)
        total = total + chunk_ref[chip].astype(F32)


def out_kernel(
    block, query_ref, within_ref, prior_ref, s0, s1, s2, s3, gain_ref, o0, o1, o2, o_own, o_far, out_ref,
    query, within, prior, state, gain, weight, normed, out, sems, out_sems,
):
    core = lax.axis_index("core")
    y = lax.axis_index("dp")
    first = [begin(prior_ref, prior, sems.at[0]), begin(gain_ref, gain, sems.at[1])]
    loads, weights = [], []
    for slot, ref in enumerate((s0, s1, s2, s3)):
        loads.append(
            [
                begin(ref.at[1 - block], state.at[slot], sems.at[2 + 3 * slot]),
                begin(query_ref.at[slot, block], query.at[slot], sems.at[3 + 3 * slot]),
                begin(within_ref.at[slot, block], within.at[slot], sems.at[4 + 3 * slot]),
            ]
        )
    for slot, ref in enumerate((o0, o1, o2)):
        weights.append(begin(ref, weight.at[pl.ds(slot * DH, DH), :], sems.at[14 + slot]))
    final = weight.at[pl.ds(3 * DH, DH), :]

    @pl.when(core == 0)
    def _():
        begin(o_own, final, sems.at[17])

    @pl.when(core != 0)
    def _():
        begin(o_far, final, sems.at[17])

    weights.append(pltpu.make_async_copy(o_own, final, sems.at[17]))
    for load in first:
        load.wait()
    share = (core if block == 0 else 1 - core).astype(F32)
    for slot in range(SLOTS):
        for load in loads[slot]:
            load.wait()
        g = gain[pl.ds(head_of(y, core, slot), 1), :]
        before = (prior[slot].astype(F32) + share * state[slot]).astype(BF16)
        mixed = within[slot] + mm(query[slot], before)
        scale = lax.rsqrt(jnp.mean(mixed * mixed, axis=-1, keepdims=True) + 1e-05)
        normed[:, slot * DH : (slot + 1) * DH] = (mixed * scale * g).astype(BF16)
    for load in weights:
        load.wait()
    copies = []
    for c in range(4):
        cols = pl.ds(c * 2 * DH, 2 * DH)
        out[:, cols] = mm(normed[...], weight[:, cols]).astype(out.dtype)
        copies.append(begin(out.at[:, cols], out_ref.at[:, cols], out_sems.at[c]))
    for copy in copies:
        copy.wait()


def body(tokens, w_query, w_key, w_value, w_out, norm_gain):
    own = tokens[0]
    key_1, value_1, query_1 = hop(w_key), hop(w_value), hop(w_query)
    other = lax.ppermute(own, "core", SWAP)

    pair = shape((2, TOK, 2 * DH), BF16)
    state = shape((2, DH, DH), F32)
    flops = 2 * 2 * TOK * D * 2 * DH
    room = [
        pltpu.VMEM((2, TOK, D), BF16),
        pltpu.VMEM((D, 2 * DH), BF16),
        pltpu.VMEM((2, TOK, 2 * DH), BF16),
        pltpu.VMEM((2, DH, DH), F32),
    ]
    one = call(key_value_kernel, 4, (pair, state), [*room, DMA((6,))], flops, 3 << 20, HBM, 16)
    last = call(
        last_key_value_kernel,
        9,
        (pair, state, shape((SLOTS, DH, DH), BF16)),
        [*room, pltpu.VMEM((3, 2, DH, DH), F32), pltpu.VMEM((SLOTS, DH, DH), BF16), DMA((10,))],
        flops,
        3 << 20,
        HBM,
        16,
    )
    barrier = lax.optimization_barrier
    kv0, s0 = one(own, other, key_1, value_1)
    key_2, value_2, query_2 = hop(key_1), hop(value_1), hop(query_1)
    key_2, value_2, query_1, s0 = barrier((key_2, value_2, query_1, s0))
    kv1, s1 = one(own, other, key_2, value_2)
    key_3, value_3, query_3 = hop(key_2), hop(value_2), hop(query_2)
    key_3, value_3, query_2, s1 = barrier((key_3, value_3, query_2, s1))
    kv2, s2 = one(own, other, key_3, value_3)
    key_4, value_4 = hop(key_3), hop(value_3)
    key_4, value_4, query_3, w_out, s2 = barrier((key_4, value_4, query_3, w_out, s2))
    query_4 = hop(query_3)
    out_1 = hop(w_out)
    kv3, s3, total = last(own, other, w_key, w_value, key_4, value_4, s0, s1, s2)
    out_1, total = barrier((out_1, total))
    out_2 = hop(out_1)

    chunks = total.reshape(CHIPS, SLOTS * DH // CHIPS, DH)
    chunks = lax.all_to_all(chunks, ("z", "x"), 0, 0, tiled=True)
    out_2, chunks = barrier((out_2, chunks))
    out_3 = hop(out_2)
    out_3, query_4 = barrier((out_3, query_4))
    out_4 = hop(out_3)
    priors = call(prefix_kernel, 1, shape(chunks.shape, BF16), [], 1 << 16, 1 << 18, VMEM, 4)(chunks)
    prior = lax.all_to_all(priors, ("z", "x"), 0, 0, tiled=True).reshape(SLOTS, DH, DH)

    queries, withins = (SLOTS, 2, TOK, DH), (SLOTS, 2, TOK, DH)
    query, within = call(
        within_kernel,
        11,
        (shape(queries, BF16), shape(withins, F32)),
        [
            pltpu.VMEM((2, TOK, D), BF16),
            pltpu.VMEM((D, SLOTS * DH), BF16),
            pltpu.VMEM((SLOTS, 2, TOK, 2 * DH), BF16),
            pltpu.VMEM(queries, BF16),
            pltpu.VMEM(withins, F32),
            DMA((14,)),
            DMA((2, SLOTS, 2)),
        ],
        3 * 2 * TOK * D * SLOTS * DH,
        8 << 20,
    )(own, other, query_1, query_2, query_3, w_query, query_4, kv0, kv1, kv2, kv3)

    operands = (query, within, prior, s0, s1, s2, s3, norm_gain.reshape(DP, DH), out_1, out_2, out_3, w_out, out_4)
    partial = []
    for block, kind in ((1, BF16), (0, F32)):
        partial.append(
            call(
                functools.partial(out_kernel, block),
                13,
                shape((TOK, D), kind),
                [
                    pltpu.VMEM((SLOTS, TOK, DH), BF16),
                    pltpu.VMEM((SLOTS, TOK, DH), F32),
                    pltpu.VMEM((SLOTS, DH, DH), BF16),
                    pltpu.VMEM((SLOTS, DH, DH), F32),
                    pltpu.VMEM((DP, DH), F32),
                    pltpu.VMEM((SLOTS * DH, D), BF16),
                    pltpu.VMEM((TOK, SLOTS * DH), BF16),
                    pltpu.VMEM((TOK, D), kind),
                    DMA((18,)),
                    DMA((4,)),
                ],
                5 << 28,
                5 << 20,
                HBM,
                16,
            )(*operands)
        )
    got = lax.ppermute(partial[0], "core", SWAP)
    return (partial[1] + got.astype(F32)).astype(BF16)[None]


def solution(mesh):
    fine = Mesh(mesh.devices.reshape(DP, ZN, XN, 2), ("dp", "z", "x", "core"))
    seq = ("z", "x", "core")
    in_specs = (
        P("dp", seq, None),
        P(None, "dp"),
        P(None, "dp"),
        P(None, "dp"),
        P("dp", None),
        P(),
    )
    return jax.shard_map(body, mesh=fine, in_specs=in_specs, out_specs=P("dp", seq, None), check_vma=False)
```

```python
import functools

import jax
import jax.numpy as jnp
from jax import lax
from jax.experimental import pallas as pl
from jax.experimental.pallas import tpu as pltpu
from jax.sharding import Mesh
from jax.sharding import PartitionSpec as P


DP, ZN, XN = 8, 8, 4
CHIPS = ZN * XN
TOK = 512
D = 1024
DH = 128
HALF = D // 2
SLOTS = 4
F32 = jnp.float32
BF16 = jnp.bfloat16
SWAP = [(0, 1), (1, 0)]
VMEM = pl.BlockSpec(memory_space=pltpu.VMEM)
HBM = pl.BlockSpec(memory_space=pl.ANY)
DMA = pltpu.SemaphoreType.DMA


def hop(weight, distance=1):
    pairs = []
    for y in range(DP):
        for place in range(2 * CHIPS):
            step = -distance if place % 2 == 0 else distance
            pairs.append((y * 2 * CHIPS + place, (y + step) % DP * 2 * CHIPS + place))
    return lax.ppermute(weight, ("dp", "z", "x", "core"), pairs)


def call(kernel, count, outs, scratch, flops, moved, spec=HBM, limit=56):
    return pl.pallas_call(
        kernel,
        out_shape=outs,
        in_specs=[spec] * count,
        out_specs=jax.tree.map(lambda _: spec, outs),
        scratch_shapes=scratch,
        compiler_params=pltpu.CompilerParams(vmem_limit_bytes=limit * 1024 * 1024),
        cost_estimate=pl.CostEstimate(flops=flops, bytes_accessed=moved, transcendentals=0),
    )


def shape(dims, kind):
    return jax.ShapeDtypeStruct(dims, kind)


def mm(a, b):
    return jnp.dot(a, b, preferred_element_type=F32)


def mm_t(a, b):
    return lax.dot_general(a, b, (((1,), (1,)), ((), ())), preferred_element_type=F32)


def t_mm(a, b):
    return lax.dot_general(a, b, (((0,), (0,)), ((), ())), preferred_element_type=F32)


def begin(source, target, sem):
    copy = pltpu.make_async_copy(source, target, sem)
    copy.start()
    return copy


def head_of(y, core, slot):
    if slot == 3:
        return lax.rem(y + 4 * core, DP)
    return lax.rem(y + DP + (slot + 1) * (1 - 2 * core), DP)


def project(own, other, loads, kv, state, tokens, weight, kv_out, state_out, sems):
    copies = [begin(ref, tokens.at[block], sems.at[2 + block]) for block, ref in enumerate((own, other))]
    for load in loads:
        load.wait()
    for block in range(2):
        copies[block].wait()
        both = mm(tokens[block], weight[...]).astype(BF16)
        kv_out[block] = both
        state_out[block] = t_mm(both[:, :DH], both[:, DH:])
    return [begin(kv_out, kv, sems.at[4]), begin(state_out, state, sems.at[5])]


def key_value_kernel(own, other, wk, wv, kv, state, tokens, weight, kv_out, state_out, sems):
    loads = [
        begin(wk, weight.at[:, pl.ds(0, DH)], sems.at[0]),
        begin(wv, weight.at[:, pl.ds(DH, DH)], sems.at[1]),
    ]
    for copy in project(own, other, loads, kv, state, tokens, weight, kv_out, state_out, sems):
        copy.wait()


def last_key_value_kernel(
    own, other, wk, wv, wk_far, wv_far, s0, s1, s2, kv, state, total, tokens, weight, kv_out, state_out, sums, total_out, sems
):
    core = lax.axis_index("core")
    left, right = weight.at[:, pl.ds(0, DH)], weight.at[:, pl.ds(DH, DH)]

    @pl.when(core == 0)
    def _():
        begin(wk, left, sems.at[0])
        begin(wv, right, sems.at[1])

    @pl.when(core != 0)
    def _():
        begin(wk_far, left, sems.at[0])
        begin(wv_far, right, sems.at[1])

    loads = [pltpu.make_async_copy(wk, left, sems.at[0]), pltpu.make_async_copy(wv, right, sems.at[1])]
    early = [begin(ref, sums.at[slot], sems.at[6 + slot]) for slot, ref in enumerate((s0, s1, s2))]
    copies = project(own, other, loads, kv, state, tokens, weight, kv_out, state_out, sems)
    for slot in range(3):
        early[slot].wait()
        total_out[slot] = (sums[slot, 0] + sums[slot, 1]).astype(BF16)
    total_out[3] = (state_out[0] + state_out[1]).astype(BF16)
    copies.append(begin(total_out, total, sems.at[9]))
    for copy in copies:
        copy.wait()


def within_kernel(
    own, other, q0, q1, q2, q_own, q_far, kv0, kv1, kv2, kv3, query_ref, within_ref,
    tokens, weight, kv, query, within, sems, out_sems,
):
    core = lax.axis_index("core")
    loads = [begin(ref, tokens.at[block], sems.at[block]) for block, ref in enumerate((own, other))]
    weights, pairs = [], []
    for slot, ref in enumerate((q0, q1, q2)):
        weights.append(begin(ref, weight.at[:, pl.ds(slot * DH, DH)], sems.at[2 + slot]))
    final = weight.at[:, pl.ds(3 * DH, DH)]

    @pl.when(core == 0)
    def _():
        begin(q_own, final, sems.at[5])

    @pl.when(core != 0)
    def _():
        begin(q_far, final, sems.at[5])

    weights.append(pltpu.make_async_copy(q_own, final, sems.at[5]))
    for slot, ref in enumerate((kv0, kv1, kv2, kv3)):
        pairs.append(begin(ref, kv.at[slot], sems.at[10 + slot]))
    half = TOK // 2
    rows = lax.broadcasted_iota(jnp.int32, (half, half), 0)
    cols = lax.broadcasted_iota(jnp.int32, (half, half), 1)
    keep = cols <= rows
    for load in loads:
        load.wait()
    copies = []
    for pair in range(2):
        for slot in (2 * pair, 2 * pair + 1):
            weights[slot].wait()
            pairs[slot].wait()
        for block in range(2):
            both = mm(tokens[block], weight[:, 2 * pair * DH : 2 * (pair + 1) * DH]).astype(BF16)
            for side in range(2):
                slot = 2 * pair + side
                q = both[:, side * DH : (side + 1) * DH]
                query[slot, block] = q
                copies.append(begin(query.at[slot, block], query_ref.at[slot, block], out_sems.at[0, slot, block]))
                key, value = kv[slot, block, :, :DH], kv[slot, block, :, DH:]
                top = jnp.where(keep, mm_t(q[:half], key[:half]), 0.0).astype(BF16)
                within[slot, block, :half] = mm(top, value[:half])
                left = mm_t(q[half:], key[:half]).astype(BF16)
                right = jnp.where(keep, mm_t(q[half:], key[half:]), 0.0).astype(BF16)
                within[slot, block, half:] = mm(left, value[:half]) + mm(right, value[half:])
                copies.append(begin(within.at[slot, block], within_ref.at[slot, block], out_sems.at[1, slot, block]))
    for copy in copies:
        copy.wait()


def prefix_kernel(chunk_ref, prior_ref):
    total = jnp.zeros(chunk_ref.shape[1:], F32)
    for chip in range(CHIPS):
        prior_ref[chip] = total.astype(BF16)
        total = total + chunk_ref[chip].astype(F32)


def out_kernel(
    block, query_ref, within_ref, prior_ref, s0, s1, s2, s3, gain_ref, o0, o1, o2, o_own, o_far, out_ref,
    query, within, prior, state, gain, weight, normed, out, sems, out_sems,
):
    core = lax.axis_index("core")
    y = lax.axis_index("dp")
    first = [begin(prior_ref, prior, sems.at[0]), begin(gain_ref, gain, sems.at[1])]
    loads, weights = [], []
    for slot, ref in enumerate((s0, s1, s2, s3)):
        loads.append(
            [
                begin(ref.at[1 - block], state.at[slot], sems.at[2 + 3 * slot]),
                begin(query_ref.at[slot, block], query.at[slot], sems.at[3 + 3 * slot]),
                begin(within_ref.at[slot, block], within.at[slot], sems.at[4 + 3 * slot]),
            ]
        )
    for slot, ref in enumerate((o0, o1, o2)):
        weights.append(begin(ref, weight.at[pl.ds(slot * DH, DH), :], sems.at[14 + slot]))
    final = weight.at[pl.ds(3 * DH, DH), :]

    @pl.when(core == 0)
    def _():
        begin(o_own, final, sems.at[17])

    @pl.when(core != 0)
    def _():
        begin(o_far, final, sems.at[17])

    weights.append(pltpu.make_async_copy(o_own, final, sems.at[17]))
    for load in first:
        load.wait()
    share = (core if block == 0 else 1 - core).astype(F32)
    for slot in range(SLOTS):
        for load in loads[slot]:
            load.wait()
        g = gain[pl.ds(head_of(y, core, slot), 1), :]
        before = (prior[slot].astype(F32) + share * state[slot]).astype(BF16)
        mixed = within[slot] + mm(query[slot], before)
        scale = lax.rsqrt(jnp.mean(mixed * mixed, axis=-1, keepdims=True) + 1e-05)
        normed[:, slot * DH : (slot + 1) * DH] = (mixed * scale * g).astype(BF16)
    for load in weights:
        load.wait()
    copies = []
    for c in range(4):
        cols = pl.ds(c * 2 * DH, 2 * DH)
        out[:, cols] = mm(normed[...], weight[:, cols]).astype(out.dtype)
        copies.append(begin(out.at[:, cols], out_ref.at[:, cols], out_sems.at[c]))
    for copy in copies:
        copy.wait()


def body(tokens, w_query, w_key, w_value, w_out, norm_gain):
    own = tokens[0]
    key_1, value_1, query_1 = hop(w_key), hop(w_value), hop(w_query)
    other = lax.ppermute(own, "core", SWAP)

    pair = shape((2, TOK, 2 * DH), BF16)
    state = shape((2, DH, DH), F32)
    flops = 2 * 2 * TOK * D * 2 * DH
    room = [
        pltpu.VMEM((2, TOK, D), BF16),
        pltpu.VMEM((D, 2 * DH), BF16),
        pltpu.VMEM((2, TOK, 2 * DH), BF16),
        pltpu.VMEM((2, DH, DH), F32),
    ]
    one = call(key_value_kernel, 4, (pair, state), [*room, DMA((6,))], flops, 3 << 20, HBM, 16)
    last = call(
        last_key_value_kernel,
        9,
        (pair, state, shape((SLOTS, DH, DH), BF16)),
        [*room, pltpu.VMEM((3, 2, DH, DH), F32), pltpu.VMEM((SLOTS, DH, DH), BF16), DMA((10,))],
        flops,
        3 << 20,
        HBM,
        16,
    )
    barrier = lax.optimization_barrier
    kv0, s0 = one(own, other, key_1, value_1)
    key_1, value_1, w_query = barrier((key_1, value_1, w_query))
    key_2, value_2 = hop(key_1), hop(value_1)
    query_2 = hop(w_query, 2)
    key_2, value_2, query_1, w_out, s0 = barrier((key_2, value_2, query_1, w_out, s0))
    kv1, s1 = one(own, other, key_2, value_2)
    key_3, value_3 = hop(key_2), hop(value_2)
    out_1 = hop(w_out)
    key_3, value_3, query_2, s1 = barrier((key_3, value_3, query_2, s1))
    kv2, s2 = one(own, other, key_3, value_3)
    key_4, value_4 = hop(key_3), hop(value_3)
    key_4, value_4, out_1, s2 = barrier((key_4, value_4, out_1, s2))
    kv3, s3, total = last(own, other, w_key, w_value, key_4, value_4, s0, s1, s2)
    w_out, s2 = barrier((w_out, s2))
    out_2 = hop(w_out, 2)
    query_3, query_4 = hop(query_2), hop(query_2, 2)
    out_3, out_4 = hop(out_2), hop(out_2, 2)

    chunks = total.reshape(CHIPS, SLOTS * DH // CHIPS, DH)
    chunks = lax.all_to_all(chunks, ("z", "x"), 0, 0, tiled=True)
    priors = call(prefix_kernel, 1, shape(chunks.shape, BF16), [], 1 << 16, 1 << 18, VMEM, 4)(chunks)
    prior = lax.all_to_all(priors, ("z", "x"), 0, 0, tiled=True).reshape(SLOTS, DH, DH)

    queries, withins = (SLOTS, 2, TOK, DH), (SLOTS, 2, TOK, DH)
    query, within = call(
        within_kernel,
        11,
        (shape(queries, BF16), shape(withins, F32)),
        [
            pltpu.VMEM((2, TOK, D), BF16),
            pltpu.VMEM((D, SLOTS * DH), BF16),
            pltpu.VMEM((SLOTS, 2, TOK, 2 * DH), BF16),
            pltpu.VMEM(queries, BF16),
            pltpu.VMEM(withins, F32),
            DMA((14,)),
            DMA((2, SLOTS, 2)),
        ],
        3 * 2 * TOK * D * SLOTS * DH,
        8 << 20,
    )(own, other, query_1, query_2, query_3, w_query, query_4, kv0, kv1, kv2, kv3)

    operands = (query, within, prior, s0, s1, s2, s3, norm_gain.reshape(DP, DH), out_1, out_2, out_3, w_out, out_4)
    partial = []
    for block, kind in ((1, BF16), (0, F32)):
        partial.append(
            call(
                functools.partial(out_kernel, block),
                13,
                shape((TOK, D), kind),
                [
                    pltpu.VMEM((SLOTS, TOK, DH), BF16),
                    pltpu.VMEM((SLOTS, TOK, DH), F32),
                    pltpu.VMEM((SLOTS, DH, DH), BF16),
                    pltpu.VMEM((SLOTS, DH, DH), F32),
                    pltpu.VMEM((DP, DH), F32),
                    pltpu.VMEM((SLOTS * DH, D), BF16),
                    pltpu.VMEM((TOK, SLOTS * DH), BF16),
                    pltpu.VMEM((TOK, D), kind),
                    DMA((18,)),
                    DMA((4,)),
                ],
                5 << 28,
                5 << 20,
                HBM,
                56,
            )(*operands)
        )
    got = lax.ppermute(partial[0], "core", SWAP)
    return (partial[1] + got.astype(F32)).astype(BF16)[None]


def solution(mesh):
    fine = Mesh(mesh.devices.reshape(DP, ZN, XN, 2), ("dp", "z", "x", "core"))
    seq = ("z", "x", "core")
    in_specs = (
        P("dp", seq, None),
        P(None, "dp"),
        P(None, "dp"),
        P(None, "dp"),
        P("dp", None),
        P(),
    )
    return jax.shard_map(body, mesh=fine, in_specs=in_specs, out_specs=P("dp", seq, None), check_vma=False)
```

```python
import functools

import jax
import jax.numpy as jnp
from jax import lax
from jax.experimental import pallas as pl
from jax.experimental.pallas import tpu as pltpu
from jax.sharding import Mesh
from jax.sharding import PartitionSpec as P


DP, ZN, XN = 8, 8, 4
CHIPS = ZN * XN
TOK = 512
D = 1024
DH = 128
HALF = D // 2
SLOTS = 4
F32 = jnp.float32
BF16 = jnp.bfloat16
SWAP = [(0, 1), (1, 0)]
VMEM = pl.BlockSpec(memory_space=pltpu.VMEM)
HBM = pl.BlockSpec(memory_space=pl.ANY)
DMA = pltpu.SemaphoreType.DMA
TOP, LOW = pl.ds(0, D), pl.ds(D, D)


def hop(weight, distance=1):
    pairs = []
    for y in range(DP):
        for place in range(2 * CHIPS):
            step = -distance if place % 2 == 0 else distance
            pairs.append((y * 2 * CHIPS + place, (y + step) % DP * 2 * CHIPS + place))
    return lax.ppermute(weight, ("dp", "z", "x", "core"), pairs)


def call(kernel, count, outs, scratch, flops, moved, spec=HBM, limit=56):
    return pl.pallas_call(
        kernel,
        out_shape=outs,
        in_specs=[spec] * count,
        out_specs=jax.tree.map(lambda _: spec, outs),
        scratch_shapes=scratch,
        compiler_params=pltpu.CompilerParams(vmem_limit_bytes=limit * 1024 * 1024),
        cost_estimate=pl.CostEstimate(flops=flops, bytes_accessed=moved, transcendentals=0),
    )


def shape(dims, kind):
    return jax.ShapeDtypeStruct(dims, kind)


def mm(a, b):
    return jnp.dot(a, b, preferred_element_type=F32)


def mm_t(a, b):
    return lax.dot_general(a, b, (((1,), (1,)), ((), ())), preferred_element_type=F32)


def t_mm(a, b):
    return lax.dot_general(a, b, (((0,), (0,)), ((), ())), preferred_element_type=F32)


def begin(source, target, sem):
    copy = pltpu.make_async_copy(source, target, sem)
    copy.start()
    return copy


def head_of(y, core, slot):
    if slot == 3:
        return lax.rem(y + 4 * core, DP)
    return lax.rem(y + DP + (slot + 1) * (1 - 2 * core), DP)


def project(own, other, loads, kv, state, tokens, weight, kv_out, state_out, sems):
    copies = [begin(ref, tokens.at[block], sems.at[2 + block]) for block, ref in enumerate((own, other))]
    for load in loads:
        load.wait()
    for block in range(2):
        copies[block].wait()
        both = mm(tokens[block], weight[...]).astype(BF16)
        kv_out[block] = both
        state_out[block] = t_mm(both[:, :DH], both[:, DH:])
    return [begin(kv_out, kv, sems.at[4]), begin(state_out, state, sems.at[5])]


def key_value_kernel(own, other, wk, wv, kv, state, tokens, weight, kv_out, state_out, sems):
    loads = [
        begin(wk, weight.at[:, pl.ds(0, DH)], sems.at[0]),
        begin(wv, weight.at[:, pl.ds(DH, DH)], sems.at[1]),
    ]
    for copy in project(own, other, loads, kv, state, tokens, weight, kv_out, state_out, sems):
        copy.wait()


def last_key_value_kernel(
    own, other, wk, wv, wk_far, wv_far, s0, s1, s2, kv, state, total, tokens, weight, kv_out, state_out, sums, total_out, sems
):
    core = lax.axis_index("core")
    left, right = weight.at[:, pl.ds(0, DH)], weight.at[:, pl.ds(DH, DH)]

    @pl.when(core == 0)
    def _():
        begin(wk, left, sems.at[0])
        begin(wv, right, sems.at[1])

    @pl.when(core != 0)
    def _():
        begin(wk_far, left, sems.at[0])
        begin(wv_far, right, sems.at[1])

    loads = [pltpu.make_async_copy(wk, left, sems.at[0]), pltpu.make_async_copy(wv, right, sems.at[1])]
    early = [begin(ref, sums.at[slot], sems.at[6 + slot]) for slot, ref in enumerate((s0, s1, s2))]
    copies = project(own, other, loads, kv, state, tokens, weight, kv_out, state_out, sems)
    for slot in range(3):
        early[slot].wait()
        total_out[slot] = (sums[slot, 0] + sums[slot, 1]).astype(BF16)
    total_out[3] = (state_out[0] + state_out[1]).astype(BF16)
    copies.append(begin(total_out, total, sems.at[9]))
    for copy in copies:
        copy.wait()


def within_kernel(
    own, other, q0, q1, q2, q_own, q_far, kv0, kv1, kv2, kv3, query_ref, within_ref,
    tokens, weight, kv, query, within, sems, out_sems,
):
    core = lax.axis_index("core")
    loads = [begin(ref, tokens.at[block], sems.at[block]) for block, ref in enumerate((own, other))]
    weights, pairs = [], []
    for slot, ref in enumerate((q0, q1, q2)):
        weights.append(begin(ref.at[TOP, :], weight.at[:, pl.ds(slot * DH, DH)], sems.at[2 + slot]))
    final = weight.at[:, pl.ds(3 * DH, DH)]

    @pl.when(core == 0)
    def _():
        begin(q_own.at[TOP, :], final, sems.at[5])

    @pl.when(core != 0)
    def _():
        begin(q_far.at[TOP, :], final, sems.at[5])

    weights.append(pltpu.make_async_copy(q_own.at[TOP, :], final, sems.at[5]))
    for slot, ref in enumerate((kv0, kv1, kv2, kv3)):
        pairs.append(begin(ref, kv.at[slot], sems.at[10 + slot]))
    half = TOK // 2
    rows = lax.broadcasted_iota(jnp.int32, (half, half), 0)
    cols = lax.broadcasted_iota(jnp.int32, (half, half), 1)
    keep = cols <= rows
    for load in loads:
        load.wait()
    copies = []
    for pair in range(2):
        for slot in (2 * pair, 2 * pair + 1):
            weights[slot].wait()
            pairs[slot].wait()
        for block in range(2):
            both = mm(tokens[block], weight[:, 2 * pair * DH : 2 * (pair + 1) * DH]).astype(BF16)
            for side in range(2):
                slot = 2 * pair + side
                q = both[:, side * DH : (side + 1) * DH]
                query[slot, block] = q
                copies.append(begin(query.at[slot, block], query_ref.at[slot, block], out_sems.at[0, slot, block]))
                key, value = kv[slot, block, :, :DH], kv[slot, block, :, DH:]
                top = jnp.where(keep, mm_t(q[:half], key[:half]), 0.0).astype(BF16)
                within[slot, block, :half] = mm(top, value[:half])
                left = mm_t(q[half:], key[:half]).astype(BF16)
                right = jnp.where(keep, mm_t(q[half:], key[half:]), 0.0).astype(BF16)
                within[slot, block, half:] = mm(left, value[:half]) + mm(right, value[half:])
                copies.append(begin(within.at[slot, block], within_ref.at[slot, block], out_sems.at[1, slot, block]))
    for copy in copies:
        copy.wait()


def prefix_kernel(chunk_ref, prior_ref):
    total = jnp.zeros(chunk_ref.shape[1:], F32)
    for chip in range(CHIPS):
        prior_ref[chip] = total.astype(BF16)
        total = total + chunk_ref[chip].astype(F32)


def out_kernel(
    block, query_ref, within_ref, prior_ref, s0, s1, s2, s3, gain_ref, o0, o1, o2, o_own, o_far, out_ref,
    query, within, prior, state, gain, weight, normed, out, sems, out_sems,
):
    core = lax.axis_index("core")
    y = lax.axis_index("dp")
    first = [begin(prior_ref, prior, sems.at[0]), begin(gain_ref, gain, sems.at[1])]
    loads, weights = [], []
    for slot, ref in enumerate((s0, s1, s2, s3)):
        loads.append(
            [
                begin(ref.at[1 - block], state.at[slot], sems.at[2 + 3 * slot]),
                begin(query_ref.at[slot, block], query.at[slot], sems.at[3 + 3 * slot]),
                begin(within_ref.at[slot, block], within.at[slot], sems.at[4 + 3 * slot]),
            ]
        )
    for slot, ref in enumerate((o0, o1, o2)):
        weights.append(begin(ref.at[LOW, :], weight.at[slot], sems.at[14 + slot]))
    final = weight.at[3]

    @pl.when(core == 0)
    def _():
        begin(o_own.at[LOW, :], final, sems.at[17])

    @pl.when(core != 0)
    def _():
        begin(o_far.at[LOW, :], final, sems.at[17])

    weights.append(pltpu.make_async_copy(o_own.at[LOW, :], final, sems.at[17]))
    for load in first:
        load.wait()
    share = (core if block == 0 else 1 - core).astype(F32)
    for slot in range(SLOTS):
        for load in loads[slot]:
            load.wait()
        g = gain[pl.ds(head_of(y, core, slot), 1), :]
        before = (prior[slot].astype(F32) + share * state[slot]).astype(BF16)
        mixed = within[slot] + mm(query[slot], before)
        scale = lax.rsqrt(jnp.mean(mixed * mixed, axis=-1, keepdims=True) + 1e-05)
        normed[:, slot * DH : (slot + 1) * DH] = (mixed * scale * g).astype(BF16)
    for load in weights:
        load.wait()
    copies = []
    for c in range(4):
        cols = pl.ds(c * 2 * DH, 2 * DH)
        tiles = [
            jnp.concatenate([weight[slot, k * DH : (k + 1) * DH, :] for slot in range(SLOTS)], axis=0)
            for k in (2 * c, 2 * c + 1)
        ]
        out[:, cols] = mm(normed[...], jnp.concatenate(tiles, axis=1)).astype(out.dtype)
        copies.append(begin(out.at[:, cols], out_ref.at[:, cols], out_sems.at[c]))
    for copy in copies:
        copy.wait()


def body(tokens, w_query, w_key, w_value, w_out, norm_gain):
    own = tokens[0]
    key_1, value_1 = hop(w_key), hop(w_value)
    other = lax.ppermute(own, "core", SWAP)

    pair = shape((2, TOK, 2 * DH), BF16)
    state = shape((2, DH, DH), F32)
    flops = 2 * 2 * TOK * D * 2 * DH
    room = [
        pltpu.VMEM((2, TOK, D), BF16),
        pltpu.VMEM((D, 2 * DH), BF16),
        pltpu.VMEM((2, TOK, 2 * DH), BF16),
        pltpu.VMEM((2, DH, DH), F32),
    ]
    one = call(key_value_kernel, 4, (pair, state), [*room, DMA((6,))], flops, 3 << 20, HBM, 16)
    last = call(
        last_key_value_kernel,
        9,
        (pair, state, shape((SLOTS, DH, DH), BF16)),
        [*room, pltpu.VMEM((3, 2, DH, DH), F32), pltpu.VMEM((SLOTS, DH, DH), BF16), DMA((10,))],
        flops,
        3 << 20,
        HBM,
        16,
    )
    barrier = lax.optimization_barrier
    blocks = w_out.reshape(DH, DP, DH).transpose(1, 0, 2).reshape(D, DH)
    pack = jnp.concatenate([w_query, blocks], axis=0)
    kv0, s0 = one(own, other, key_1, value_1)
    key_2, value_2 = hop(key_1), hop(value_1)
    pack_1 = hop(pack)
    key_2, value_2, s0 = barrier((key_2, value_2, s0))
    kv1, s1 = one(own, other, key_2, value_2)
    key_3, value_3 = hop(key_2), hop(value_2)
    pack_1, key_3 = barrier((pack_1, key_3))
    pack_2 = hop(pack_1)
    key_3, value_3, s1 = barrier((key_3, value_3, s1))
    kv2, s2 = one(own, other, key_3, value_3)
    key_4, value_4 = hop(key_3), hop(value_3)
    pack_2, key_4, value_4, s2 = barrier((pack_2, key_4, value_4, s2))
    pack_3 = hop(pack_2)
    kv3, s3, total = last(own, other, w_key, w_value, key_4, value_4, s0, s1, s2)

    chunks = total.reshape(CHIPS, SLOTS * DH // CHIPS, DH)
    chunks = lax.all_to_all(chunks, ("z", "x"), 0, 0, tiled=True)
    pack_3, chunks = barrier((pack_3, chunks))
    pack_4 = hop(pack_3)
    priors = call(prefix_kernel, 1, shape(chunks.shape, BF16), [], 1 << 16, 1 << 18, VMEM, 4)(chunks)
    prior = lax.all_to_all(priors, ("z", "x"), 0, 0, tiled=True).reshape(SLOTS, DH, DH)

    queries, withins = (SLOTS, 2, TOK, DH), (SLOTS, 2, TOK, DH)
    query, within = call(
        within_kernel,
        11,
        (shape(queries, BF16), shape(withins, F32)),
        [
            pltpu.VMEM((2, TOK, D), BF16),
            pltpu.VMEM((D, SLOTS * DH), BF16),
            pltpu.VMEM((SLOTS, 2, TOK, 2 * DH), BF16),
            pltpu.VMEM(queries, BF16),
            pltpu.VMEM(withins, F32),
            DMA((14,)),
            DMA((2, SLOTS, 2)),
        ],
        3 * 2 * TOK * D * SLOTS * DH,
        8 << 20,
    )(own, other, pack_1, pack_2, pack_3, pack, pack_4, kv0, kv1, kv2, kv3)

    operands = (query, within, prior, s0, s1, s2, s3, norm_gain.reshape(DP, DH), pack_1, pack_2, pack_3, pack, pack_4)
    partial = []
    for block, kind, limit in ((1, BF16, 56), (0, F32, 56)):
        partial.append(
            call(
                functools.partial(out_kernel, block),
                13,
                shape((TOK, D), kind),
                [
                    pltpu.VMEM((SLOTS, TOK, DH), BF16),
                    pltpu.VMEM((SLOTS, TOK, DH), F32),
                    pltpu.VMEM((SLOTS, DH, DH), BF16),
                    pltpu.VMEM((SLOTS, DH, DH), F32),
                    pltpu.VMEM((DP, DH), F32),
                    pltpu.VMEM((SLOTS, D, DH), BF16),
                    pltpu.VMEM((TOK, SLOTS * DH), BF16),
                    pltpu.VMEM((TOK, D), kind),
                    DMA((18,)),
                    DMA((4,)),
                ],
                5 << 28,
                5 << 20,
                HBM,
                limit,
            )(*operands)
        )
    got = lax.ppermute(partial[0], "core", SWAP)
    return (partial[1] + got.astype(F32)).astype(BF16)[None]


def solution(mesh):
    fine = Mesh(mesh.devices.reshape(DP, ZN, XN, 2), ("dp", "z", "x", "core"))
    seq = ("z", "x", "core")
    in_specs = (
        P("dp", seq, None),
        P(None, "dp"),
        P(None, "dp"),
        P(None, "dp"),
        P("dp", None),
        P(),
    )
    return jax.shard_map(body, mesh=fine, in_specs=in_specs, out_specs=P("dp", seq, None), check_vma=False)
```

```python
import functools

import jax
import jax.numpy as jnp
from jax import lax
from jax.experimental import pallas as pl
from jax.experimental.pallas import tpu as pltpu
from jax.sharding import Mesh
from jax.sharding import PartitionSpec as P


DP, ZN, XN = 8, 8, 4
CHIPS = ZN * XN
TOK = 512
D = 1024
DH = 128
HALF = D // 2
SLOTS = 4
F32 = jnp.float32
BF16 = jnp.bfloat16
SWAP = [(0, 1), (1, 0)]
VMEM = pl.BlockSpec(memory_space=pltpu.VMEM)
HBM = pl.BlockSpec(memory_space=pl.ANY)
DMA = pltpu.SemaphoreType.DMA
TOP, LOW = pl.ds(0, D), pl.ds(D, D)


def hop(weight, distance=1):
    pairs = []
    for y in range(DP):
        for place in range(2 * CHIPS):
            step = -distance if place % 2 == 0 else distance
            pairs.append((y * 2 * CHIPS + place, (y + step) % DP * 2 * CHIPS + place))
    return lax.ppermute(weight, ("dp", "z", "x", "core"), pairs)


def call(kernel, count, outs, scratch, flops, moved, spec=HBM, limit=56):
    return pl.pallas_call(
        kernel,
        out_shape=outs,
        in_specs=[spec] * count,
        out_specs=jax.tree.map(lambda _: spec, outs),
        scratch_shapes=scratch,
        compiler_params=pltpu.CompilerParams(vmem_limit_bytes=limit * 1024 * 1024),
        cost_estimate=pl.CostEstimate(flops=flops, bytes_accessed=moved, transcendentals=0),
    )


def shape(dims, kind):
    return jax.ShapeDtypeStruct(dims, kind)


def mm(a, b):
    return jnp.dot(a, b, preferred_element_type=F32)


def mm_t(a, b):
    return lax.dot_general(a, b, (((1,), (1,)), ((), ())), preferred_element_type=F32)


def t_mm(a, b):
    return lax.dot_general(a, b, (((0,), (0,)), ((), ())), preferred_element_type=F32)


def begin(source, target, sem):
    copy = pltpu.make_async_copy(source, target, sem)
    copy.start()
    return copy


def head_of(y, core, slot):
    if slot == 3:
        return lax.rem(y + 4 * core, DP)
    return lax.rem(y + DP + (slot + 1) * (1 - 2 * core), DP)


def project(own, other, loads, kv, state, tokens, weight, kv_out, state_out, sems):
    copies = [begin(ref, tokens.at[block], sems.at[2 + block]) for block, ref in enumerate((own, other))]
    for load in loads:
        load.wait()
    for block in range(2):
        copies[block].wait()
        both = mm(tokens[block], weight[...]).astype(BF16)
        kv_out[block] = both
        state_out[block] = t_mm(both[:, :DH], both[:, DH:])
    return [begin(kv_out, kv, sems.at[4]), begin(state_out, state, sems.at[5])]


def key_value_kernel(own, other, wk, wv, kv, state, tokens, weight, kv_out, state_out, sems):
    loads = [
        begin(wk, weight.at[:, pl.ds(0, DH)], sems.at[0]),
        begin(wv, weight.at[:, pl.ds(DH, DH)], sems.at[1]),
    ]
    for copy in project(own, other, loads, kv, state, tokens, weight, kv_out, state_out, sems):
        copy.wait()


def last_key_value_kernel(
    own, other, wk, wv, wk_far, wv_far, s0, s1, s2, kv, state, total, tokens, weight, kv_out, state_out, sums, total_out, sems
):
    core = lax.axis_index("core")
    left, right = weight.at[:, pl.ds(0, DH)], weight.at[:, pl.ds(DH, DH)]

    @pl.when(core == 0)
    def _():
        begin(wk, left, sems.at[0])
        begin(wv, right, sems.at[1])

    @pl.when(core != 0)
    def _():
        begin(wk_far, left, sems.at[0])
        begin(wv_far, right, sems.at[1])

    loads = [pltpu.make_async_copy(wk, left, sems.at[0]), pltpu.make_async_copy(wv, right, sems.at[1])]
    early = [begin(ref, sums.at[slot], sems.at[6 + slot]) for slot, ref in enumerate((s0, s1, s2))]
    copies = project(own, other, loads, kv, state, tokens, weight, kv_out, state_out, sems)
    for slot in range(3):
        early[slot].wait()
        total_out[slot] = (sums[slot, 0] + sums[slot, 1]).astype(BF16)
    total_out[3] = (state_out[0] + state_out[1]).astype(BF16)
    copies.append(begin(total_out, total, sems.at[9]))
    for copy in copies:
        copy.wait()


def within_kernel(final, *refs):
    count = 7 if final else 6
    own, other, *packs = refs[: count - 2]
    kvs = refs[count - 2 : count]
    query_ref, within_ref, tokens, weight, kv, query, within, sems, out_sems = refs[count:]
    core = lax.axis_index("core")
    loads = [begin(ref, tokens.at[block], sems.at[block]) for block, ref in enumerate((own, other))]
    left, right = weight.at[:, pl.ds(0, DH)], weight.at[:, pl.ds(DH, DH)]
    loads.append(begin(packs[0].at[TOP, :], left, sems.at[2]))
    if final:

        @pl.when(core == 0)
        def _():
            begin(packs[1].at[TOP, :], right, sems.at[3])

        @pl.when(core != 0)
        def _():
            begin(packs[2].at[TOP, :], right, sems.at[3])

        loads.append(pltpu.make_async_copy(packs[1].at[TOP, :], right, sems.at[3]))
    else:
        loads.append(begin(packs[1].at[TOP, :], right, sems.at[3]))
    pairs = [begin(ref, kv.at[side], sems.at[4 + side]) for side, ref in enumerate(kvs)]
    half = TOK // 2
    rows = lax.broadcasted_iota(jnp.int32, (half, half), 0)
    cols = lax.broadcasted_iota(jnp.int32, (half, half), 1)
    keep = cols <= rows
    for index in (0, 2, 3):
        loads[index].wait()
    copies = []
    for block in range(2):
        if block == 1:
            loads[1].wait()
        both = mm(tokens[block], weight[...]).astype(BF16)
        for side in range(2):
            if block == 0:
                pairs[side].wait()
            q = both[:, side * DH : (side + 1) * DH]
            query[side, block] = q
            copies.append(begin(query.at[side, block], query_ref.at[side, block], out_sems.at[0, side, block]))
            key, value = kv[side, block, :, :DH], kv[side, block, :, DH:]
            top = jnp.where(keep, mm_t(q[:half], key[:half]), 0.0).astype(BF16)
            within[side, block, :half] = mm(top, value[:half])
            low = mm_t(q[half:], key[:half]).astype(BF16)
            corner = jnp.where(keep, mm_t(q[half:], key[half:]), 0.0).astype(BF16)
            within[side, block, half:] = mm(low, value[:half]) + mm(corner, value[half:])
            copies.append(begin(within.at[side, block], within_ref.at[side, block], out_sems.at[1, side, block]))
    for copy in copies:
        copy.wait()


def prefix_kernel(chunk_ref, prior_ref):
    total = jnp.zeros(chunk_ref.shape[1:], F32)
    for chip in range(CHIPS):
        prior_ref[chip] = total.astype(BF16)
        total = total + chunk_ref[chip].astype(F32)


def out_kernel(
    block, query_a, query_b, within_a, within_b, prior_ref, s0, s1, s2, s3, gain_ref, o0, o1, o2, o_own, o_far, out_ref,
    query, within, prior, state, gain, weight, normed, out, sems, out_sems,
):
    core = lax.axis_index("core")
    y = lax.axis_index("dp")
    first = [begin(prior_ref, prior, sems.at[0]), begin(gain_ref, gain, sems.at[1])]
    loads, weights = [], []
    for slot, ref in enumerate((s0, s1, s2, s3)):
        loads.append(
            [
                begin(ref.at[1 - block], state.at[slot], sems.at[2 + 3 * slot]),
                begin((query_a, query_b)[slot // 2].at[slot % 2, block], query.at[slot], sems.at[3 + 3 * slot]),
                begin((within_a, within_b)[slot // 2].at[slot % 2, block], within.at[slot], sems.at[4 + 3 * slot]),
            ]
        )
    for slot, ref in enumerate((o0, o1, o2)):
        weights.append(begin(ref.at[LOW, :], weight.at[slot], sems.at[14 + slot]))
    final = weight.at[3]

    @pl.when(core == 0)
    def _():
        begin(o_own.at[LOW, :], final, sems.at[17])

    @pl.when(core != 0)
    def _():
        begin(o_far.at[LOW, :], final, sems.at[17])

    weights.append(pltpu.make_async_copy(o_own.at[LOW, :], final, sems.at[17]))
    for load in first:
        load.wait()
    share = (core if block == 0 else 1 - core).astype(F32)
    for slot in range(SLOTS):
        for load in loads[slot]:
            load.wait()
        g = gain[pl.ds(head_of(y, core, slot), 1), :]
        before = (prior[slot].astype(F32) + share * state[slot]).astype(BF16)
        mixed = within[slot] + mm(query[slot], before)
        scale = lax.rsqrt(jnp.mean(mixed * mixed, axis=-1, keepdims=True) + 1e-05)
        normed[:, slot * DH : (slot + 1) * DH] = (mixed * scale * g).astype(BF16)
    for load in weights:
        load.wait()
    copies = []
    for c in range(4):
        cols = pl.ds(c * 2 * DH, 2 * DH)
        tiles = [
            jnp.concatenate([weight[slot, k * DH : (k + 1) * DH, :] for slot in range(SLOTS)], axis=0)
            for k in (2 * c, 2 * c + 1)
        ]
        out[:, cols] = mm(normed[...], jnp.concatenate(tiles, axis=1)).astype(out.dtype)
        copies.append(begin(out.at[:, cols], out_ref.at[:, cols], out_sems.at[c]))
    for copy in copies:
        copy.wait()


def body(tokens, w_query, w_key, w_value, w_out, norm_gain):
    own = tokens[0]
    key_1, value_1 = hop(w_key), hop(w_value)
    other = lax.ppermute(own, "core", SWAP)

    pair = shape((2, TOK, 2 * DH), BF16)
    state = shape((2, DH, DH), F32)
    flops = 2 * 2 * TOK * D * 2 * DH
    room = [
        pltpu.VMEM((2, TOK, D), BF16),
        pltpu.VMEM((D, 2 * DH), BF16),
        pltpu.VMEM((2, TOK, 2 * DH), BF16),
        pltpu.VMEM((2, DH, DH), F32),
    ]
    one = call(key_value_kernel, 4, (pair, state), [*room, DMA((6,))], flops, 3 << 20, HBM, 16)
    last = call(
        last_key_value_kernel,
        9,
        (pair, state, shape((SLOTS, DH, DH), BF16)),
        [*room, pltpu.VMEM((3, 2, DH, DH), F32), pltpu.VMEM((SLOTS, DH, DH), BF16), DMA((10,))],
        flops,
        3 << 20,
        HBM,
        16,
    )
    barrier = lax.optimization_barrier
    blocks = w_out.reshape(DH, DP, DH).transpose(1, 0, 2).reshape(D, DH)
    pack = jnp.concatenate([w_query, blocks], axis=0)
    kv0, s0 = one(own, other, key_1, value_1)
    key_2, value_2 = hop(key_1), hop(value_1)
    pack_1 = hop(pack)
    key_2, value_2, s0 = barrier((key_2, value_2, s0))
    kv1, s1 = one(own, other, key_2, value_2)
    key_3, value_3 = hop(key_2), hop(value_2)
    pack_1, key_3 = barrier((pack_1, key_3))
    pack_2 = hop(pack_1)
    key_3, value_3, s1 = barrier((key_3, value_3, s1))
    kv2, s2 = one(own, other, key_3, value_3)
    key_4, value_4 = hop(key_3), hop(value_3)
    key_4, value_4, s2 = barrier((key_4, value_4, s2))
    kv3, s3, total = last(own, other, w_key, w_value, key_4, value_4, s0, s1, s2)
    pack_3, pack_4 = hop(pack_2), hop(pack_2, 2)

    half = (2, 2, TOK, DH)

    def attend(final, *arrays):
        return call(
            functools.partial(within_kernel, final),
            len(arrays),
            (shape(half, BF16), shape(half, F32)),
            [
                pltpu.VMEM((2, TOK, D), BF16),
                pltpu.VMEM((D, 2 * DH), BF16),
                pltpu.VMEM((2, 2, TOK, 2 * DH), BF16),
                pltpu.VMEM(half, BF16),
                pltpu.VMEM(half, F32),
                DMA((6,)),
                DMA((2, 2, 2)),
            ],
            3 * TOK * D * SLOTS * DH,
            5 << 20,
        )(*arrays)

    query_a, within_a = attend(False, own, other, pack_1, pack_2, kv0, kv1)

    chunks = total.reshape(CHIPS, SLOTS * DH // CHIPS, DH)
    chunks = lax.all_to_all(chunks, ("z", "x"), 0, 0, tiled=True)
    chunks, query_a = barrier((chunks, query_a))
    priors = call(prefix_kernel, 1, shape(chunks.shape, BF16), [], 1 << 16, 1 << 18, VMEM, 4)(chunks)
    prior = lax.all_to_all(priors, ("z", "x"), 0, 0, tiled=True).reshape(SLOTS, DH, DH)

    query_b, within_b = attend(True, own, other, pack_3, pack, pack_4, kv2, kv3)

    operands = (query_a, query_b, within_a, within_b, prior, s0, s1, s2, s3, norm_gain.reshape(DP, DH), pack_1, pack_2, pack_3, pack, pack_4)
    partial = []
    for block, kind, limit in ((1, BF16, 56), (0, BF16, 56)):
        partial.append(
            call(
                functools.partial(out_kernel, block),
                15,
                shape((TOK, D), kind),
                [
                    pltpu.VMEM((SLOTS, TOK, DH), BF16),
                    pltpu.VMEM((SLOTS, TOK, DH), F32),
                    pltpu.VMEM((SLOTS, DH, DH), BF16),
                    pltpu.VMEM((SLOTS, DH, DH), F32),
                    pltpu.VMEM((DP, DH), F32),
                    pltpu.VMEM((SLOTS, D, DH), BF16),
                    pltpu.VMEM((TOK, SLOTS * DH), BF16),
                    pltpu.VMEM((TOK, D), kind),
                    DMA((18,)),
                    DMA((4,)),
                ],
                5 << 28,
                5 << 20,
                HBM,
                limit,
            )(*operands)
        )
    got = lax.ppermute(partial[0], "core", SWAP)
    return (partial[1].astype(F32) + got.astype(F32)).astype(BF16)[None]


def solution(mesh):
    fine = Mesh(mesh.devices.reshape(DP, ZN, XN, 2), ("dp", "z", "x", "core"))
    seq = ("z", "x", "core")
    in_specs = (
        P("dp", seq, None),
        P(None, "dp"),
        P(None, "dp"),
        P(None, "dp"),
        P("dp", None),
        P(),
    )
    return jax.shard_map(body, mesh=fine, in_specs=in_specs, out_specs=P("dp", seq, None), check_vma=False)
```

```python
import functools

import jax
import jax.numpy as jnp
from jax import lax
from jax.experimental import pallas as pl
from jax.experimental.pallas import tpu as pltpu
from jax.sharding import Mesh
from jax.sharding import PartitionSpec as P


DP, ZN, XN = 8, 8, 4
CHIPS = ZN * XN
TOK = 512
D = 1024
DH = 128
HALF = D // 2
SLOTS = 4
F32 = jnp.float32
BF16 = jnp.bfloat16
SWAP = [(0, 1), (1, 0)]
VMEM = pl.BlockSpec(memory_space=pltpu.VMEM)
HBM = pl.BlockSpec(memory_space=pl.ANY)
DMA = pltpu.SemaphoreType.DMA
TOP, LOW = pl.ds(0, D), pl.ds(D, D)


def hop(weight, distance=1):
    pairs = []
    for y in range(DP):
        for place in range(2 * CHIPS):
            step = -distance if place % 2 == 0 else distance
            pairs.append((y * 2 * CHIPS + place, (y + step) % DP * 2 * CHIPS + place))
    return lax.ppermute(weight, ("dp", "z", "x", "core"), pairs)


def call(kernel, count, outs, scratch, flops, moved, spec=HBM, limit=56):
    return pl.pallas_call(
        kernel,
        out_shape=outs,
        in_specs=[spec] * count,
        out_specs=jax.tree.map(lambda _: spec, outs),
        scratch_shapes=scratch,
        compiler_params=pltpu.CompilerParams(vmem_limit_bytes=limit * 1024 * 1024),
        cost_estimate=pl.CostEstimate(flops=flops, bytes_accessed=moved, transcendentals=0),
    )


def shape(dims, kind):
    return jax.ShapeDtypeStruct(dims, kind)


def mm(a, b):
    return jnp.dot(a, b, preferred_element_type=F32)


def mm_t(a, b):
    return lax.dot_general(a, b, (((1,), (1,)), ((), ())), preferred_element_type=F32)


def t_mm(a, b):
    return lax.dot_general(a, b, (((0,), (0,)), ((), ())), preferred_element_type=F32)


def begin(source, target, sem):
    copy = pltpu.make_async_copy(source, target, sem)
    copy.start()
    return copy


def head_of(y, core, slot):
    if slot == 3:
        return lax.rem(y + 4 * core, DP)
    return lax.rem(y + DP + (slot + 1) * (1 - 2 * core), DP)


def project(own, other, loads, kv, state, tokens, weight, kv_out, state_out, sems):
    copies = [begin(ref, tokens.at[block], sems.at[2 + block]) for block, ref in enumerate((own, other))]
    for load in loads:
        load.wait()
    for block in range(2):
        copies[block].wait()
        both = mm(tokens[block], weight[...]).astype(BF16)
        kv_out[block] = both
        state_out[block] = t_mm(both[:, :DH], both[:, DH:])
    return [begin(kv_out, kv, sems.at[4]), begin(state_out, state, sems.at[5])]


def key_value_kernel(own, other, wk, wv, kv, state, tokens, weight, kv_out, state_out, sems):
    loads = [
        begin(wk, weight.at[:, pl.ds(0, DH)], sems.at[0]),
        begin(wv, weight.at[:, pl.ds(DH, DH)], sems.at[1]),
    ]
    for copy in project(own, other, loads, kv, state, tokens, weight, kv_out, state_out, sems):
        copy.wait()


def last_key_value_kernel(
    own, other, wk, wv, wk_far, wv_far, s0, s1, s2, kv, state, total, tokens, weight, kv_out, state_out, sums, total_out, sems
):
    core = lax.axis_index("core")
    left, right = weight.at[:, pl.ds(0, DH)], weight.at[:, pl.ds(DH, DH)]

    @pl.when(core == 0)
    def _():
        begin(wk, left, sems.at[0])
        begin(wv, right, sems.at[1])

    @pl.when(core != 0)
    def _():
        begin(wk_far, left, sems.at[0])
        begin(wv_far, right, sems.at[1])

    loads = [pltpu.make_async_copy(wk, left, sems.at[0]), pltpu.make_async_copy(wv, right, sems.at[1])]
    early = [begin(ref, sums.at[slot], sems.at[6 + slot]) for slot, ref in enumerate((s0, s1, s2))]
    copies = project(own, other, loads, kv, state, tokens, weight, kv_out, state_out, sems)
    for slot in range(3):
        early[slot].wait()
        total_out[slot] = (sums[slot, 0] + sums[slot, 1]).astype(BF16)
    total_out[3] = (state_out[0] + state_out[1]).astype(BF16)
    copies.append(begin(total_out, total, sems.at[9]))
    for copy in copies:
        copy.wait()


def within_kernel(final, *refs):
    count = 7 if final else 6
    own, other, *packs = refs[: count - 2]
    kvs = refs[count - 2 : count]
    query_ref, within_ref, tokens, weight, kv, query, within, sems, out_sems = refs[count:]
    core = lax.axis_index("core")
    loads = [begin(ref, tokens.at[block], sems.at[block]) for block, ref in enumerate((own, other))]
    left, right = weight.at[:, pl.ds(0, DH)], weight.at[:, pl.ds(DH, DH)]
    loads.append(begin(packs[0].at[TOP, :], left, sems.at[2]))
    if final:

        @pl.when(core == 0)
        def _():
            begin(packs[1].at[TOP, :], right, sems.at[3])

        @pl.when(core != 0)
        def _():
            begin(packs[2].at[TOP, :], right, sems.at[3])

        loads.append(pltpu.make_async_copy(packs[1].at[TOP, :], right, sems.at[3]))
    else:
        loads.append(begin(packs[1].at[TOP, :], right, sems.at[3]))
    pairs = [begin(ref, kv.at[side], sems.at[4 + side]) for side, ref in enumerate(kvs)]
    half = TOK // 2
    rows = lax.broadcasted_iota(jnp.int32, (half, half), 0)
    cols = lax.broadcasted_iota(jnp.int32, (half, half), 1)
    keep = cols <= rows
    for index in (0, 2, 3):
        loads[index].wait()
    copies = []
    for block in range(2):
        if block == 1:
            loads[1].wait()
        both = mm(tokens[block], weight[...]).astype(BF16)
        for side in range(2):
            if block == 0:
                pairs[side].wait()
            q = both[:, side * DH : (side + 1) * DH]
            query[side, block] = q
            copies.append(begin(query.at[side, block], query_ref.at[side, block], out_sems.at[0, side, block]))
            key, value = kv[side, block, :, :DH], kv[side, block, :, DH:]
            top = jnp.where(keep, mm_t(q[:half], key[:half]), 0.0).astype(BF16)
            within[side, block, :half] = mm(top, value[:half])
            low = mm_t(q[half:], key[:half]).astype(BF16)
            corner = jnp.where(keep, mm_t(q[half:], key[half:]), 0.0).astype(BF16)
            within[side, block, half:] = mm(low, value[:half]) + mm(corner, value[half:])
            copies.append(begin(within.at[side, block], within_ref.at[side, block], out_sems.at[1, side, block]))
    for copy in copies:
        copy.wait()


def prefix_kernel(chunk_ref, prior_ref):
    total = jnp.zeros(chunk_ref.shape[1:], F32)
    for chip in range(CHIPS):
        prior_ref[chip] = total.astype(BF16)
        total = total + chunk_ref[chip].astype(F32)


def out_kernel(
    block, query_a, query_b, within_a, within_b, prior_ref, s0, s1, s2, s3, gain_ref, o0, o1, o2, o_own, o_far, out_ref,
    query, within, prior, state, gain, weight, normed, out, sems, out_sems,
):
    core = lax.axis_index("core")
    y = lax.axis_index("dp")
    first = [begin(prior_ref, prior, sems.at[0]), begin(gain_ref, gain, sems.at[1])]
    loads, weights = [], []
    for slot, ref in enumerate((s0, s1, s2, s3)):
        loads.append(
            [
                begin(ref.at[1 - block], state.at[slot], sems.at[2 + 3 * slot]),
                begin((query_a, query_b)[slot // 2].at[slot % 2, block], query.at[slot], sems.at[3 + 3 * slot]),
                begin((within_a, within_b)[slot // 2].at[slot % 2, block], within.at[slot], sems.at[4 + 3 * slot]),
            ]
        )
    for slot, ref in enumerate((o0, o1, o2)):
        weights.append(begin(ref.at[LOW, :], weight.at[slot], sems.at[14 + slot]))
    final = weight.at[3]

    @pl.when(core == 0)
    def _():
        begin(o_own.at[LOW, :], final, sems.at[17])

    @pl.when(core != 0)
    def _():
        begin(o_far.at[LOW, :], final, sems.at[17])

    weights.append(pltpu.make_async_copy(o_own.at[LOW, :], final, sems.at[17]))
    for load in first:
        load.wait()
    share = (core if block == 0 else 1 - core).astype(F32)
    for slot in range(SLOTS):
        for load in loads[slot]:
            load.wait()
        g = gain[pl.ds(head_of(y, core, slot), 1), :]
        before = (prior[slot].astype(F32) + share * state[slot]).astype(BF16)
        mixed = within[slot] + mm(query[slot], before)
        scale = lax.rsqrt(jnp.mean(mixed * mixed, axis=-1, keepdims=True) + 1e-05)
        normed[:, slot * DH : (slot + 1) * DH] = (mixed * scale * g).astype(BF16)
    for load in weights:
        load.wait()
    copies = []
    for c in range(4):
        cols = pl.ds(c * 2 * DH, 2 * DH)
        tiles = [
            jnp.concatenate([weight[slot, k * DH : (k + 1) * DH, :] for slot in range(SLOTS)], axis=0)
            for k in (2 * c, 2 * c + 1)
        ]
        out[:, cols] = mm(normed[...], jnp.concatenate(tiles, axis=1)).astype(out.dtype)
        copies.append(begin(out.at[:, cols], out_ref.at[:, cols], out_sems.at[c]))
    for copy in copies:
        copy.wait()


def body(tokens, w_query, w_key, w_value, w_out, norm_gain):
    own = tokens[0]
    key_1, value_1 = hop(w_key), hop(w_value)
    other = lax.ppermute(own, "core", SWAP)

    pair = shape((2, TOK, 2 * DH), BF16)
    state = shape((2, DH, DH), F32)
    flops = 2 * 2 * TOK * D * 2 * DH
    room = [
        pltpu.VMEM((2, TOK, D), BF16),
        pltpu.VMEM((D, 2 * DH), BF16),
        pltpu.VMEM((2, TOK, 2 * DH), BF16),
        pltpu.VMEM((2, DH, DH), F32),
    ]
    one = call(key_value_kernel, 4, (pair, state), [*room, DMA((6,))], flops, 3 << 20, HBM, 16)
    last = call(
        last_key_value_kernel,
        9,
        (pair, state, shape((SLOTS, DH, DH), BF16)),
        [*room, pltpu.VMEM((3, 2, DH, DH), F32), pltpu.VMEM((SLOTS, DH, DH), BF16), DMA((10,))],
        flops,
        3 << 20,
        HBM,
        16,
    )
    barrier = lax.optimization_barrier
    blocks = w_out.reshape(DH, DP, DH).transpose(1, 0, 2).reshape(D, DH)
    pack = jnp.concatenate([w_query, blocks], axis=0)
    kv0, s0 = one(own, other, key_1, value_1)
    key_2, value_2 = hop(key_1), hop(value_1)
    pack_1 = hop(pack)
    key_2, value_2, s0 = barrier((key_2, value_2, s0))
    kv1, s1 = one(own, other, key_2, value_2)
    key_3, value_3 = hop(key_2), hop(value_2)
    pack_1, key_3 = barrier((pack_1, key_3))
    pack_2 = hop(pack_1)
    key_3, value_3, s1 = barrier((key_3, value_3, s1))
    kv2, s2 = one(own, other, key_3, value_3)
    key_4, value_4 = hop(key_3), hop(value_3)
    pack_2, key_4, value_4, s2 = barrier((pack_2, key_4, value_4, s2))
    kv3, s3, total = last(own, other, w_key, w_value, key_4, value_4, s0, s1, s2)
    pack_2, total = barrier((pack_2, total))
    pack_3, pack_4 = hop(pack_2), hop(pack_2, 2)

    half = (2, 2, TOK, DH)

    def attend(final, *arrays):
        return call(
            functools.partial(within_kernel, final),
            len(arrays),
            (shape(half, BF16), shape(half, F32)),
            [
                pltpu.VMEM((2, TOK, D), BF16),
                pltpu.VMEM((D, 2 * DH), BF16),
                pltpu.VMEM((2, 2, TOK, 2 * DH), BF16),
                pltpu.VMEM(half, BF16),
                pltpu.VMEM(half, F32),
                DMA((6,)),
                DMA((2, 2, 2)),
            ],
            3 * TOK * D * SLOTS * DH,
            5 << 20,
        )(*arrays)

    query_a, within_a = attend(False, own, other, pack_1, pack_2, kv0, kv1)

    chunks = total.reshape(CHIPS, SLOTS * DH // CHIPS, DH)
    chunks = lax.all_to_all(chunks, ("z", "x"), 0, 0, tiled=True)
    chunks, query_a = barrier((chunks, query_a))
    priors = call(prefix_kernel, 1, shape(chunks.shape, BF16), [], 1 << 16, 1 << 18, VMEM, 4)(chunks)
    prior = lax.all_to_all(priors, ("z", "x"), 0, 0, tiled=True).reshape(SLOTS, DH, DH)

    query_b, within_b = attend(True, own, other, pack_3, pack, pack_4, kv2, kv3)

    operands = (query_a, query_b, within_a, within_b, prior, s0, s1, s2, s3, norm_gain.reshape(DP, DH), pack_1, pack_2, pack_3, pack, pack_4)
    partial = []
    for block, kind, limit in ((1, BF16, 56), (0, BF16, 56)):
        partial.append(
            call(
                functools.partial(out_kernel, block),
                15,
                shape((TOK, D), kind),
                [
                    pltpu.VMEM((SLOTS, TOK, DH), BF16),
                    pltpu.VMEM((SLOTS, TOK, DH), F32),
                    pltpu.VMEM((SLOTS, DH, DH), BF16),
                    pltpu.VMEM((SLOTS, DH, DH), F32),
                    pltpu.VMEM((DP, DH), F32),
                    pltpu.VMEM((SLOTS, D, DH), BF16),
                    pltpu.VMEM((TOK, SLOTS * DH), BF16),
                    pltpu.VMEM((TOK, D), kind),
                    DMA((18,)),
                    DMA((4,)),
                ],
                5 << 28,
                5 << 20,
                HBM,
                limit,
            )(*operands)
        )
    got = lax.ppermute(partial[0], "core", SWAP)
    return (partial[1].astype(F32) + got.astype(F32)).astype(BF16)[None]


def solution(mesh):
    fine = Mesh(mesh.devices.reshape(DP, ZN, XN, 2), ("dp", "z", "x", "core"))
    seq = ("z", "x", "core")
    in_specs = (
        P("dp", seq, None),
        P(None, "dp"),
        P(None, "dp"),
        P(None, "dp"),
        P("dp", None),
        P(),
    )
    return jax.shard_map(body, mesh=fine, in_specs=in_specs, out_specs=P("dp", seq, None), check_vma=False)
```

```python
import functools

import jax
import jax.numpy as jnp
from jax import lax
from jax.experimental import pallas as pl
from jax.experimental.pallas import tpu as pltpu
from jax.sharding import Mesh
from jax.sharding import PartitionSpec as P


DP, ZN, XN = 8, 8, 4
CHIPS = ZN * XN
TOK = 512
D = 1024
DH = 128
HALF = D // 2
SLOTS = 4
F32 = jnp.float32
BF16 = jnp.bfloat16
SWAP = [(0, 1), (1, 0)]
VMEM = pl.BlockSpec(memory_space=pltpu.VMEM)
HBM = pl.BlockSpec(memory_space=pl.ANY)
DMA = pltpu.SemaphoreType.DMA
TOP, LOW = pl.ds(0, D), pl.ds(D, D)


def hop(weight, distance=1):
    pairs = []
    for y in range(DP):
        for place in range(2 * CHIPS):
            step = -distance if place % 2 == 0 else distance
            pairs.append((y * 2 * CHIPS + place, (y + step) % DP * 2 * CHIPS + place))
    return lax.ppermute(weight, ("dp", "z", "x", "core"), pairs)


def call(kernel, count, outs, scratch, flops, moved, spec=HBM, limit=56):
    return pl.pallas_call(
        kernel,
        out_shape=outs,
        in_specs=[spec] * count,
        out_specs=jax.tree.map(lambda _: spec, outs),
        scratch_shapes=scratch,
        compiler_params=pltpu.CompilerParams(vmem_limit_bytes=limit * 1024 * 1024),
        cost_estimate=pl.CostEstimate(flops=flops, bytes_accessed=moved, transcendentals=0),
    )


def shape(dims, kind):
    return jax.ShapeDtypeStruct(dims, kind)


def mm(a, b):
    return jnp.dot(a, b, preferred_element_type=F32)


def mm_t(a, b):
    return lax.dot_general(a, b, (((1,), (1,)), ((), ())), preferred_element_type=F32)


def t_mm(a, b):
    return lax.dot_general(a, b, (((0,), (0,)), ((), ())), preferred_element_type=F32)


def begin(source, target, sem):
    copy = pltpu.make_async_copy(source, target, sem)
    copy.start()
    return copy


def head_of(y, core, slot):
    if slot == 3:
        return lax.rem(y + 4 * core, DP)
    return lax.rem(y + DP + (slot + 1) * (1 - 2 * core), DP)


def project(tokens, weight, kv, state):
    for block, ref in enumerate(tokens):
        both = mm(ref[...], weight).astype(BF16)
        kv[block] = both
        state[block] = t_mm(both[:, :DH], both[:, DH:])


def key_value_kernel(own, other, wk, wv, kv, state):
    project((own, other), jnp.concatenate([wk[...], wv[...]], axis=1), kv, state)


def last_key_value_kernel(own, other, wk, wv, wk_far, wv_far, s0, s1, s2, kv, state, total):
    first = lax.axis_index("core") == 0
    weight = [jnp.where(first, wk[...], wk_far[...]), jnp.where(first, wv[...], wv_far[...])]
    project((own, other), jnp.concatenate(weight, axis=1), kv, state)
    for slot, ref in enumerate((s0, s1, s2, state)):
        total[slot] = (ref[0] + ref[1]).astype(BF16)


def within_kernel(final, *refs):
    count = 7 if final else 6
    own, other, *packs = refs[: count - 2]
    kvs = refs[count - 2 : count]
    query_ref, within_ref, tokens, weight, kv, query, within, sems, out_sems = refs[count:]
    core = lax.axis_index("core")
    loads = [begin(ref, tokens.at[block], sems.at[block]) for block, ref in enumerate((own, other))]
    left, right = weight.at[:, pl.ds(0, DH)], weight.at[:, pl.ds(DH, DH)]
    loads.append(begin(packs[0].at[TOP, :], left, sems.at[2]))
    if final:

        @pl.when(core == 0)
        def _():
            begin(packs[1].at[TOP, :], right, sems.at[3])

        @pl.when(core != 0)
        def _():
            begin(packs[2].at[TOP, :], right, sems.at[3])

        loads.append(pltpu.make_async_copy(packs[1].at[TOP, :], right, sems.at[3]))
    else:
        loads.append(begin(packs[1].at[TOP, :], right, sems.at[3]))
    pairs = [begin(ref, kv.at[side], sems.at[4 + side]) for side, ref in enumerate(kvs)]
    half = TOK // 2
    rows = lax.broadcasted_iota(jnp.int32, (half, half), 0)
    cols = lax.broadcasted_iota(jnp.int32, (half, half), 1)
    keep = cols <= rows
    for index in (0, 2, 3):
        loads[index].wait()
    copies = []
    for block in range(2):
        if block == 1:
            loads[1].wait()
        both = mm(tokens[block], weight[...]).astype(BF16)
        for side in range(2):
            if block == 0:
                pairs[side].wait()
            q = both[:, side * DH : (side + 1) * DH]
            query[side, block] = q
            copies.append(begin(query.at[side, block], query_ref.at[side, block], out_sems.at[0, side, block]))
            key, value = kv[side, block, :, :DH], kv[side, block, :, DH:]
            top = jnp.where(keep, mm_t(q[:half], key[:half]), 0.0).astype(BF16)
            within[side, block, :half] = mm(top, value[:half])
            low = mm_t(q[half:], key[:half]).astype(BF16)
            corner = jnp.where(keep, mm_t(q[half:], key[half:]), 0.0).astype(BF16)
            within[side, block, half:] = mm(low, value[:half]) + mm(corner, value[half:])
            copies.append(begin(within.at[side, block], within_ref.at[side, block], out_sems.at[1, side, block]))
    for copy in copies:
        copy.wait()


def prefix_kernel(chunk_ref, prior_ref):
    total = jnp.zeros(chunk_ref.shape[1:], F32)
    for chip in range(CHIPS):
        prior_ref[chip] = total.astype(BF16)
        total = total + chunk_ref[chip].astype(F32)


def out_kernel(
    block, query_a, query_b, within_a, within_b, prior_ref, s0, s1, s2, s3, gain_ref, o0, o1, o2, o_own, o_far, out_ref,
    query, within, prior, state, gain, weight, normed, out, sems, out_sems,
):
    core = lax.axis_index("core")
    y = lax.axis_index("dp")
    first = [begin(prior_ref, prior, sems.at[0]), begin(gain_ref, gain, sems.at[1])]
    loads, weights = [], []
    for slot, ref in enumerate((s0, s1, s2, s3)):
        loads.append(
            [
                begin(ref.at[1 - block], state.at[slot], sems.at[2 + 3 * slot]),
                begin((query_a, query_b)[slot // 2].at[slot % 2, block], query.at[slot], sems.at[3 + 3 * slot]),
                begin((within_a, within_b)[slot // 2].at[slot % 2, block], within.at[slot], sems.at[4 + 3 * slot]),
            ]
        )
    for slot, ref in enumerate((o0, o1, o2)):
        weights.append(begin(ref.at[LOW, :], weight.at[slot], sems.at[14 + slot]))
    final = weight.at[3]

    @pl.when(core == 0)
    def _():
        begin(o_own.at[LOW, :], final, sems.at[17])

    @pl.when(core != 0)
    def _():
        begin(o_far.at[LOW, :], final, sems.at[17])

    weights.append(pltpu.make_async_copy(o_own.at[LOW, :], final, sems.at[17]))
    for load in first:
        load.wait()
    share = (core if block == 0 else 1 - core).astype(F32)
    for slot in range(SLOTS):
        for load in loads[slot]:
            load.wait()
        g = gain[pl.ds(head_of(y, core, slot), 1), :]
        before = (prior[slot].astype(F32) + share * state[slot]).astype(BF16)
        mixed = within[slot] + mm(query[slot], before)
        scale = lax.rsqrt(jnp.mean(mixed * mixed, axis=-1, keepdims=True) + 1e-05)
        normed[:, slot * DH : (slot + 1) * DH] = (mixed * scale * g).astype(BF16)
    for load in weights:
        load.wait()
    copies = []
    for c in range(4):
        cols = pl.ds(c * 2 * DH, 2 * DH)
        tiles = [
            jnp.concatenate([weight[slot, k * DH : (k + 1) * DH, :] for slot in range(SLOTS)], axis=0)
            for k in (2 * c, 2 * c + 1)
        ]
        out[:, cols] = mm(normed[...], jnp.concatenate(tiles, axis=1)).astype(out.dtype)
        copies.append(begin(out.at[:, cols], out_ref.at[:, cols], out_sems.at[c]))
    for copy in copies:
        copy.wait()


def body(tokens, w_query, w_key, w_value, w_out, norm_gain):
    own = tokens[0]
    key_1, value_1 = hop(w_key), hop(w_value)
    other = lax.ppermute(own, "core", SWAP)

    pair = shape((2, TOK, 2 * DH), BF16)
    state = shape((2, DH, DH), F32)
    flops = 2 * 2 * TOK * D * 2 * DH
    one = call(key_value_kernel, 4, (pair, state), [], flops, 3 << 20, VMEM, 16)
    outs = (pair, state, shape((SLOTS, DH, DH), BF16))
    last = call(last_key_value_kernel, 9, outs, [], flops, 3 << 20, VMEM, 16)

    barrier = lax.optimization_barrier
    blocks = w_out.reshape(DH, DP, DH).transpose(1, 0, 2).reshape(D, DH)
    pack = jnp.concatenate([w_query, blocks], axis=0)
    kv0, s0 = one(own, other, key_1, value_1)
    key_2, value_2 = hop(key_1), hop(value_1)
    pack_1 = hop(pack)
    key_2, value_2, s0 = barrier((key_2, value_2, s0))
    kv1, s1 = one(own, other, key_2, value_2)
    key_3, value_3 = hop(key_2), hop(value_2)
    pack_1, key_3 = barrier((pack_1, key_3))
    pack_2 = hop(pack_1)
    key_3, value_3, s1 = barrier((key_3, value_3, s1))
    kv2, s2 = one(own, other, key_3, value_3)
    key_4, value_4 = hop(key_3), hop(value_3)
    pack_2, key_4, value_4, s2 = barrier((pack_2, key_4, value_4, s2))
    kv3, s3, total = last(own, other, w_key, w_value, key_4, value_4, s0, s1, s2)
    pack_2, total = barrier((pack_2, total))
    pack_3, pack_4 = hop(pack_2), hop(pack_2, 2)

    half = (2, 2, TOK, DH)

    def attend(final, *arrays):
        return call(
            functools.partial(within_kernel, final),
            len(arrays),
            (shape(half, BF16), shape(half, F32)),
            [
                pltpu.VMEM((2, TOK, D), BF16),
                pltpu.VMEM((D, 2 * DH), BF16),
                pltpu.VMEM((2, 2, TOK, 2 * DH), BF16),
                pltpu.VMEM(half, BF16),
                pltpu.VMEM(half, F32),
                DMA((6,)),
                DMA((2, 2, 2)),
            ],
            3 * TOK * D * SLOTS * DH,
            5 << 20,
        )(*arrays)

    query_a, within_a = attend(False, own, other, pack_1, pack_2, kv0, kv1)

    chunks = total.reshape(CHIPS, SLOTS * DH // CHIPS, DH)
    chunks = lax.all_to_all(chunks, ("z", "x"), 0, 0, tiled=True)
    chunks, query_a = barrier((chunks, query_a))
    priors = call(prefix_kernel, 1, shape(chunks.shape, BF16), [], 1 << 16, 1 << 18, VMEM, 4)(chunks)
    prior = lax.all_to_all(priors, ("z", "x"), 0, 0, tiled=True).reshape(SLOTS, DH, DH)

    query_b, within_b = attend(True, own, other, pack_3, pack, pack_4, kv2, kv3)

    operands = (query_a, query_b, within_a, within_b, prior, s0, s1, s2, s3, norm_gain.reshape(DP, DH), pack_1, pack_2, pack_3, pack, pack_4)
    partial = []
    for block, kind, limit in ((1, BF16, 56), (0, BF16, 56)):
        partial.append(
            call(
                functools.partial(out_kernel, block),
                15,
                shape((TOK, D), kind),
                [
                    pltpu.VMEM((SLOTS, TOK, DH), BF16),
                    pltpu.VMEM((SLOTS, TOK, DH), F32),
                    pltpu.VMEM((SLOTS, DH, DH), BF16),
                    pltpu.VMEM((SLOTS, DH, DH), F32),
                    pltpu.VMEM((DP, DH), F32),
                    pltpu.VMEM((SLOTS, D, DH), BF16),
                    pltpu.VMEM((TOK, SLOTS * DH), BF16),
                    pltpu.VMEM((TOK, D), kind),
                    DMA((18,)),
                    DMA((4,)),
                ],
                5 << 28,
                5 << 20,
                HBM,
                limit,
            )(*operands)
        )
    got = lax.ppermute(partial[0], "core", SWAP)
    return (partial[1].astype(F32) + got.astype(F32)).astype(BF16)[None]


def solution(mesh):
    fine = Mesh(mesh.devices.reshape(DP, ZN, XN, 2), ("dp", "z", "x", "core"))
    seq = ("z", "x", "core")
    in_specs = (
        P("dp", seq, None),
        P(None, "dp"),
        P(None, "dp"),
        P(None, "dp"),
        P("dp", None),
        P(),
    )
    return jax.shard_map(body, mesh=fine, in_specs=in_specs, out_specs=P("dp", seq, None), check_vma=False)
```

```python
import functools

import jax
import jax.numpy as jnp
from jax import lax
from jax.experimental import pallas as pl
from jax.experimental.pallas import tpu as pltpu
from jax.sharding import Mesh
from jax.sharding import PartitionSpec as P


DP, ZN, XN = 8, 8, 4
CHIPS = ZN * XN
TOK = 512
D = 1024
DH = 128
HALF = D // 2
SLOTS = 4
F32 = jnp.float32
BF16 = jnp.bfloat16
SWAP = [(0, 1), (1, 0)]
VMEM = pl.BlockSpec(memory_space=pltpu.VMEM)
HBM = pl.BlockSpec(memory_space=pl.ANY)
DMA = pltpu.SemaphoreType.DMA
TOP, LOW = pl.ds(0, D), pl.ds(D, D)


def hop(weight, distance=1):
    pairs = []
    for y in range(DP):
        for place in range(2 * CHIPS):
            step = -distance if place % 2 == 0 else distance
            pairs.append((y * 2 * CHIPS + place, (y + step) % DP * 2 * CHIPS + place))
    return lax.ppermute(weight, ("dp", "z", "x", "core"), pairs)


def call(kernel, count, outs, scratch, flops, moved, spec=HBM, limit=56):
    return pl.pallas_call(
        kernel,
        out_shape=outs,
        in_specs=[spec] * count,
        out_specs=jax.tree.map(lambda _: spec, outs),
        scratch_shapes=scratch,
        compiler_params=pltpu.CompilerParams(vmem_limit_bytes=limit * 1024 * 1024),
        cost_estimate=pl.CostEstimate(flops=flops, bytes_accessed=moved, transcendentals=0),
    )


def shape(dims, kind):
    return jax.ShapeDtypeStruct(dims, kind)


def mm(a, b):
    return jnp.dot(a, b, preferred_element_type=F32)


def mm_t(a, b):
    return lax.dot_general(a, b, (((1,), (1,)), ((), ())), preferred_element_type=F32)


def t_mm(a, b):
    return lax.dot_general(a, b, (((0,), (0,)), ((), ())), preferred_element_type=F32)


def begin(source, target, sem):
    copy = pltpu.make_async_copy(source, target, sem)
    copy.start()
    return copy


def head_of(y, core, slot):
    if slot == 3:
        return lax.rem(y + 4 * core, DP)
    return lax.rem(y + DP + (slot + 1) * (1 - 2 * core), DP)


def project(tokens, weight, kv, state):
    for block, ref in enumerate(tokens):
        both = mm(ref[...], weight).astype(BF16)
        kv[block] = both
        state[block] = t_mm(both[:, :DH], both[:, DH:])


def key_value_kernel(own, other, wk, wv, kv, state):
    project((own, other), jnp.concatenate([wk[...], wv[...]], axis=1), kv, state)


def last_key_value_kernel(own, other, wk, wv, wk_far, wv_far, s0, s1, s2, kv, state, total):
    first = lax.axis_index("core") == 0
    weight = [jnp.where(first, wk[...], wk_far[...]), jnp.where(first, wv[...], wv_far[...])]
    project((own, other), jnp.concatenate(weight, axis=1), kv, state)
    for slot, ref in enumerate((s0, s1, s2, state)):
        total[slot] = (ref[0] + ref[1]).astype(BF16)


def within_kernel(final, *refs):
    count = 7 if final else 6
    own, other, *packs = refs[: count - 2]
    kvs = refs[count - 2 : count]
    query_ref, within_ref, tokens, weight, kv, query, within, sems, out_sems = refs[count:]
    core = lax.axis_index("core")
    loads = [begin(ref, tokens.at[block], sems.at[block]) for block, ref in enumerate((own, other))]
    left, right = weight.at[:, pl.ds(0, DH)], weight.at[:, pl.ds(DH, DH)]
    loads.append(begin(packs[0].at[TOP, :], left, sems.at[2]))
    if final:

        @pl.when(core == 0)
        def _():
            begin(packs[1].at[TOP, :], right, sems.at[3])

        @pl.when(core != 0)
        def _():
            begin(packs[2].at[TOP, :], right, sems.at[3])

        loads.append(pltpu.make_async_copy(packs[1].at[TOP, :], right, sems.at[3]))
    else:
        loads.append(begin(packs[1].at[TOP, :], right, sems.at[3]))
    pairs = [begin(ref, kv.at[side], sems.at[4 + side]) for side, ref in enumerate(kvs)]
    half = TOK // 2
    rows = lax.broadcasted_iota(jnp.int32, (half, half), 0)
    cols = lax.broadcasted_iota(jnp.int32, (half, half), 1)
    keep = cols <= rows
    for index in (0, 2, 3):
        loads[index].wait()
    copies = []
    for block in range(2):
        if block == 1:
            loads[1].wait()
        both = mm(tokens[block], weight[...]).astype(BF16)
        for side in range(2):
            if block == 0:
                pairs[side].wait()
            q = both[:, side * DH : (side + 1) * DH]
            query[side, block] = q
            copies.append(begin(query.at[side, block], query_ref.at[side, block], out_sems.at[0, side, block]))
            key, value = kv[side, block, :, :DH], kv[side, block, :, DH:]
            top = jnp.where(keep, mm_t(q[:half], key[:half]), 0.0).astype(BF16)
            within[side, block, :half] = mm(top, value[:half])
            low = mm_t(q[half:], key[:half]).astype(BF16)
            corner = jnp.where(keep, mm_t(q[half:], key[half:]), 0.0).astype(BF16)
            within[side, block, half:] = mm(low, value[:half]) + mm(corner, value[half:])
            copies.append(begin(within.at[side, block], within_ref.at[side, block], out_sems.at[1, side, block]))
    for copy in copies:
        copy.wait()


def prefix_kernel(chunk_ref, prior_ref):
    total = jnp.zeros(chunk_ref.shape[1:], F32)
    for chip in range(CHIPS):
        prior_ref[chip] = total.astype(BF16)
        total = total + chunk_ref[chip].astype(F32)


def out_kernel(
    block, query_a, query_b, within_a, within_b, prior_ref, s0, s1, s2, s3, gain_ref, o0, o1, o2, o_own, o_far, out_ref,
    query, within, prior, state, gain, weight, normed, out, sems, out_sems,
):
    core = lax.axis_index("core")
    y = lax.axis_index("dp")
    first = [begin(prior_ref, prior, sems.at[0]), begin(gain_ref, gain, sems.at[1])]
    loads, weights = [], []
    for slot, ref in enumerate((s0, s1, s2, s3)):
        loads.append(
            [
                begin(ref.at[1 - block], state.at[slot], sems.at[2 + 3 * slot]),
                begin((query_a, query_b)[slot // 2].at[slot % 2, block], query.at[slot], sems.at[3 + 3 * slot]),
                begin((within_a, within_b)[slot // 2].at[slot % 2, block], within.at[slot], sems.at[4 + 3 * slot]),
            ]
        )
    for slot, ref in enumerate((o0, o1, o2)):
        weights.append(begin(ref.at[LOW, :], weight.at[slot], sems.at[14 + slot]))
    final = weight.at[3]

    @pl.when(core == 0)
    def _():
        begin(o_own.at[LOW, :], final, sems.at[17])

    @pl.when(core != 0)
    def _():
        begin(o_far.at[LOW, :], final, sems.at[17])

    weights.append(pltpu.make_async_copy(o_own.at[LOW, :], final, sems.at[17]))
    for load in first:
        load.wait()
    share = (core if block == 0 else 1 - core).astype(F32)
    for slot in range(SLOTS):
        for load in loads[slot]:
            load.wait()
        g = gain[pl.ds(head_of(y, core, slot), 1), :]
        before = (prior[slot].astype(F32) + share * state[slot]).astype(BF16)
        mixed = within[slot] + mm(query[slot], before)
        scale = lax.rsqrt(jnp.mean(mixed * mixed, axis=-1, keepdims=True) + 1e-05)
        normed[:, slot * DH : (slot + 1) * DH] = (mixed * scale * g).astype(BF16)
    for load in weights:
        load.wait()
    copies = []
    for c in range(4):
        cols = pl.ds(c * 2 * DH, 2 * DH)
        tiles = [
            jnp.concatenate([weight[slot, k * DH : (k + 1) * DH, :] for slot in range(SLOTS)], axis=0)
            for k in (2 * c, 2 * c + 1)
        ]
        out[:, cols] = mm(normed[...], jnp.concatenate(tiles, axis=1)).astype(out.dtype)
        copies.append(begin(out.at[:, cols], out_ref.at[:, cols], out_sems.at[c]))
    for copy in copies:
        copy.wait()


def body(tokens, w_query, w_key, w_value, w_out, norm_gain):
    own = tokens[0]
    key_1, value_1 = hop(w_key), hop(w_value)
    other = lax.ppermute(own, "core", SWAP)

    pair = shape((2, TOK, 2 * DH), BF16)
    state = shape((2, DH, DH), F32)
    flops = 2 * 2 * TOK * D * 2 * DH
    one = call(key_value_kernel, 4, (pair, state), [], flops, 3 << 20, VMEM, 16)
    outs = (pair, state, shape((SLOTS, DH, DH), BF16))
    last = call(last_key_value_kernel, 9, outs, [], flops, 3 << 20, VMEM, 16)

    barrier = lax.optimization_barrier
    blocks = w_out.reshape(DH, DP, DH).transpose(1, 0, 2).reshape(D, DH)
    pack = jnp.concatenate([w_query, blocks], axis=0)
    kv0, s0 = one(own, other, key_1, value_1)
    key_2, value_2 = hop(key_1), hop(value_1)
    pack_1 = hop(pack)
    key_2, value_2, s0 = barrier((key_2, value_2, s0))
    kv1, s1 = one(own, other, key_2, value_2)
    key_3, value_3 = hop(key_2), hop(value_2)
    pack_1, key_3, value_3 = barrier((pack_1, key_3, value_3))
    pack_2 = hop(pack_1)
    key_3, value_3, s1 = barrier((key_3, value_3, s1))
    kv2, s2 = one(own, other, key_3, value_3)
    key_4, value_4 = hop(key_3), hop(value_3)
    pack_2, s2 = barrier((pack_2, s2))
    pack_3, pack_4 = hop(pack_2), hop(pack_2, 2)
    pack_2, key_4, value_4, s2 = barrier((pack_2, key_4, value_4, s2))
    kv3, s3, total = last(own, other, w_key, w_value, key_4, value_4, s0, s1, s2)

    half = (2, 2, TOK, DH)

    def attend(final, *arrays):
        return call(
            functools.partial(within_kernel, final),
            len(arrays),
            (shape(half, BF16), shape(half, F32)),
            [
                pltpu.VMEM((2, TOK, D), BF16),
                pltpu.VMEM((D, 2 * DH), BF16),
                pltpu.VMEM((2, 2, TOK, 2 * DH), BF16),
                pltpu.VMEM(half, BF16),
                pltpu.VMEM(half, F32),
                DMA((6,)),
                DMA((2, 2, 2)),
            ],
            3 * TOK * D * SLOTS * DH,
            5 << 20,
        )(*arrays)

    query_a, within_a = attend(False, own, other, pack_1, pack_2, kv0, kv1)

    chunks = total.reshape(CHIPS, SLOTS * DH // CHIPS, DH)
    chunks = lax.all_to_all(chunks, ("z", "x"), 0, 0, tiled=True)
    chunks, query_a = barrier((chunks, query_a))
    priors = call(prefix_kernel, 1, shape(chunks.shape, BF16), [], 1 << 16, 1 << 18, VMEM, 4)(chunks)
    prior = lax.all_to_all(priors, ("z", "x"), 0, 0, tiled=True).reshape(SLOTS, DH, DH)

    query_b, within_b = attend(True, own, other, pack_3, pack, pack_4, kv2, kv3)

    operands = (query_a, query_b, within_a, within_b, prior, s0, s1, s2, s3, norm_gain.reshape(DP, DH), pack_1, pack_2, pack_3, pack, pack_4)
    partial = []
    for block, kind, limit in ((1, BF16, 56), (0, BF16, 56)):
        partial.append(
            call(
                functools.partial(out_kernel, block),
                15,
                shape((TOK, D), kind),
                [
                    pltpu.VMEM((SLOTS, TOK, DH), BF16),
                    pltpu.VMEM((SLOTS, TOK, DH), F32),
                    pltpu.VMEM((SLOTS, DH, DH), BF16),
                    pltpu.VMEM((SLOTS, DH, DH), F32),
                    pltpu.VMEM((DP, DH), F32),
                    pltpu.VMEM((SLOTS, D, DH), BF16),
                    pltpu.VMEM((TOK, SLOTS * DH), BF16),
                    pltpu.VMEM((TOK, D), kind),
                    DMA((18,)),
                    DMA((4,)),
                ],
                5 << 28,
                5 << 20,
                HBM,
                limit,
            )(*operands)
        )
    got = lax.ppermute(partial[0], "core", SWAP)
    return (partial[1].astype(F32) + got.astype(F32)).astype(BF16)[None]


def solution(mesh):
    fine = Mesh(mesh.devices.reshape(DP, ZN, XN, 2), ("dp", "z", "x", "core"))
    seq = ("z", "x", "core")
    in_specs = (
        P("dp", seq, None),
        P(None, "dp"),
        P(None, "dp"),
        P(None, "dp"),
        P("dp", None),
        P(),
    )
    return jax.shard_map(body, mesh=fine, in_specs=in_specs, out_specs=P("dp", seq, None), check_vma=False)
```

```python
import functools

import jax
import jax.numpy as jnp
from jax import lax
from jax.experimental import pallas as pl
from jax.experimental.pallas import tpu as pltpu
from jax.sharding import Mesh
from jax.sharding import PartitionSpec as P


DP, ZN, XN = 8, 8, 4
CHIPS = ZN * XN
TOK = 512
D = 1024
DH = 128
HALF = D // 2
SLOTS = 4
F32 = jnp.float32
BF16 = jnp.bfloat16
SWAP = [(0, 1), (1, 0)]
VMEM = pl.BlockSpec(memory_space=pltpu.VMEM)
HBM = pl.BlockSpec(memory_space=pl.ANY)
DMA = pltpu.SemaphoreType.DMA
TOP, LOW = pl.ds(0, D), pl.ds(D, D)


def hop(weight, distance=1):
    pairs = []
    for y in range(DP):
        for place in range(2 * CHIPS):
            step = -distance if place % 2 == 0 else distance
            pairs.append((y * 2 * CHIPS + place, (y + step) % DP * 2 * CHIPS + place))
    return lax.ppermute(weight, ("dp", "z", "x", "core"), pairs)


def call(kernel, count, outs, scratch, flops, moved, spec=HBM, limit=56):
    return pl.pallas_call(
        kernel,
        out_shape=outs,
        in_specs=[spec] * count,
        out_specs=jax.tree.map(lambda _: spec, outs),
        scratch_shapes=scratch,
        compiler_params=pltpu.CompilerParams(vmem_limit_bytes=limit * 1024 * 1024),
        cost_estimate=pl.CostEstimate(flops=flops, bytes_accessed=moved, transcendentals=0),
    )


def shape(dims, kind):
    return jax.ShapeDtypeStruct(dims, kind)


def mm(a, b):
    return jnp.dot(a, b, preferred_element_type=F32)


def mm_t(a, b):
    return lax.dot_general(a, b, (((1,), (1,)), ((), ())), preferred_element_type=F32)


def t_mm(a, b):
    return lax.dot_general(a, b, (((0,), (0,)), ((), ())), preferred_element_type=F32)


def begin(source, target, sem):
    copy = pltpu.make_async_copy(source, target, sem)
    copy.start()
    return copy


def head_of(y, core, slot):
    if slot == 3:
        return lax.rem(y + 4 * core, DP)
    return lax.rem(y + DP + (slot + 1) * (1 - 2 * core), DP)


def project(tokens, weight, kv, state):
    for block, ref in enumerate(tokens):
        both = mm(ref[...], weight).astype(BF16)
        kv[block] = both
        state[block] = t_mm(both[:, :DH], both[:, DH:])


def key_value_kernel(own, other, wk, wv, kv, state):
    project((own, other), jnp.concatenate([wk[...], wv[...]], axis=1), kv, state)


def last_key_value_kernel(own, other, wk, wv, wk_far, wv_far, s0, s1, s2, kv, state, total):
    first = lax.axis_index("core") == 0
    weight = [jnp.where(first, wk[...], wk_far[...]), jnp.where(first, wv[...], wv_far[...])]
    project((own, other), jnp.concatenate(weight, axis=1), kv, state)
    for slot, ref in enumerate((s0, s1, s2, state)):
        total[slot] = (ref[0] + ref[1]).astype(BF16)


def within_kernel(final, *refs):
    count = 7 if final else 6
    own, other, *packs = refs[: count - 2]
    kvs = refs[count - 2 : count]
    query_ref, within_ref, tokens, weight, kv, query, within, sems, out_sems = refs[count:]
    core = lax.axis_index("core")
    loads = [begin(ref, tokens.at[block], sems.at[block]) for block, ref in enumerate((own, other))]
    left, right = weight.at[:, pl.ds(0, DH)], weight.at[:, pl.ds(DH, DH)]
    loads.append(begin(packs[0].at[TOP, :], left, sems.at[2]))
    if final:

        @pl.when(core == 0)
        def _():
            begin(packs[1].at[TOP, :], right, sems.at[3])

        @pl.when(core != 0)
        def _():
            begin(packs[2].at[TOP, :], right, sems.at[3])

        loads.append(pltpu.make_async_copy(packs[1].at[TOP, :], right, sems.at[3]))
    else:
        loads.append(begin(packs[1].at[TOP, :], right, sems.at[3]))
    pairs = [begin(ref, kv.at[side], sems.at[4 + side]) for side, ref in enumerate(kvs)]
    half = TOK // 2
    rows = lax.broadcasted_iota(jnp.int32, (half, half), 0)
    cols = lax.broadcasted_iota(jnp.int32, (half, half), 1)
    keep = cols <= rows
    for index in (0, 2, 3):
        loads[index].wait()
    copies = []
    for block in range(2):
        if block == 1:
            loads[1].wait()
        both = mm(tokens[block], weight[...]).astype(BF16)
        for side in range(2):
            if block == 0:
                pairs[side].wait()
            q = both[:, side * DH : (side + 1) * DH]
            query[side, block] = q
            copies.append(begin(query.at[side, block], query_ref.at[side, block], out_sems.at[0, side, block]))
            key, value = kv[side, block, :, :DH], kv[side, block, :, DH:]
            top = jnp.where(keep, mm_t(q[:half], key[:half]), 0.0).astype(BF16)
            within[side, block, :half] = mm(top, value[:half])
            low = mm_t(q[half:], key[:half]).astype(BF16)
            corner = jnp.where(keep, mm_t(q[half:], key[half:]), 0.0).astype(BF16)
            within[side, block, half:] = mm(low, value[:half]) + mm(corner, value[half:])
            copies.append(begin(within.at[side, block], within_ref.at[side, block], out_sems.at[1, side, block]))
    for copy in copies:
        copy.wait()


def prefix_kernel(chunk_ref, prior_ref):
    total = jnp.zeros(chunk_ref.shape[1:], F32)
    for chip in range(CHIPS):
        prior_ref[chip] = total.astype(BF16)
        total = total + chunk_ref[chip].astype(F32)


def out_kernel(
    block, query_a, query_b, within_a, within_b, prior_ref, s0, s1, s2, s3, gain_ref, o0, o1, o2, o_own, o_far, out_ref,
    query, within, prior, state, gain, weight, normed, out, sems, out_sems,
):
    core = lax.axis_index("core")
    y = lax.axis_index("dp")
    first = [begin(prior_ref, prior, sems.at[0]), begin(gain_ref, gain, sems.at[1])]
    loads, weights = [], []
    for slot, ref in enumerate((s0, s1, s2, s3)):
        loads.append(
            [
                begin(ref.at[1 - block], state.at[slot], sems.at[2 + 3 * slot]),
                begin((query_a, query_b)[slot // 2].at[slot % 2, block], query.at[slot], sems.at[3 + 3 * slot]),
                begin((within_a, within_b)[slot // 2].at[slot % 2, block], within.at[slot], sems.at[4 + 3 * slot]),
            ]
        )
    for slot, ref in enumerate((o0, o1, o2)):
        weights.append(begin(ref.at[LOW, :], weight.at[slot], sems.at[14 + slot]))
    final = weight.at[3]

    @pl.when(core == 0)
    def _():
        begin(o_own.at[LOW, :], final, sems.at[17])

    @pl.when(core != 0)
    def _():
        begin(o_far.at[LOW, :], final, sems.at[17])

    weights.append(pltpu.make_async_copy(o_own.at[LOW, :], final, sems.at[17]))
    for load in first:
        load.wait()
    share = (core if block == 0 else 1 - core).astype(F32)
    for slot in range(SLOTS):
        for load in loads[slot]:
            load.wait()
        g = gain[pl.ds(head_of(y, core, slot), 1), :]
        before = (prior[slot].astype(F32) + share * state[slot]).astype(BF16)
        mixed = within[slot] + mm(query[slot], before)
        scale = lax.rsqrt(jnp.mean(mixed * mixed, axis=-1, keepdims=True) + 1e-05)
        normed[:, slot * DH : (slot + 1) * DH] = (mixed * scale * g).astype(BF16)
    for load in weights:
        load.wait()
    copies = []
    for c in range(4):
        cols = pl.ds(c * 2 * DH, 2 * DH)
        tiles = [
            jnp.concatenate([weight[slot, k * DH : (k + 1) * DH, :] for slot in range(SLOTS)], axis=0)
            for k in (2 * c, 2 * c + 1)
        ]
        out[:, cols] = mm(normed[...], jnp.concatenate(tiles, axis=1)).astype(out.dtype)
        copies.append(begin(out.at[:, cols], out_ref.at[:, cols], out_sems.at[c]))
    for copy in copies:
        copy.wait()


def body(tokens, w_query, w_key, w_value, w_out, norm_gain):
    own = tokens[0]
    key_1, value_1 = hop(w_key), hop(w_value)
    other = lax.ppermute(own, "core", SWAP)

    pair = shape((2, TOK, 2 * DH), BF16)
    state = shape((2, DH, DH), F32)
    flops = 2 * 2 * TOK * D * 2 * DH
    one = call(key_value_kernel, 4, (pair, state), [], flops, 3 << 20, VMEM, 16)
    outs = (pair, state, shape((SLOTS, DH, DH), BF16))
    last = call(last_key_value_kernel, 9, outs, [], flops, 3 << 20, VMEM, 16)

    barrier = lax.optimization_barrier
    blocks = w_out.reshape(DH, DP, DH).transpose(1, 0, 2).reshape(D, DH)
    pack = jnp.concatenate([w_query, blocks], axis=0)
    kv0, s0 = one(own, other, key_1, value_1)
    key_2, value_2 = hop(key_1), hop(value_1)
    pack_1 = hop(pack)
    key_2, value_2, s0 = barrier((key_2, value_2, s0))
    kv1, s1 = one(own, other, key_2, value_2)
    key_3, value_3 = hop(key_2), hop(value_2)
    pack_1, key_3, value_3, s1 = barrier((pack_1, key_3, value_3, s1))
    pack_2 = hop(pack_1)
    key_3, value_3, s1 = barrier((key_3, value_3, s1))
    kv2, s2 = one(own, other, key_3, value_3)
    key_4, value_4 = hop(key_3), hop(value_3)
    pack_2, s2 = barrier((pack_2, s2))
    pack_3, pack_4 = hop(pack_2), hop(pack_2, 2)
    pack_2, key_4, value_4, s2 = barrier((pack_2, key_4, value_4, s2))
    kv3, s3, total = last(own, other, w_key, w_value, key_4, value_4, s0, s1, s2)

    half = (2, 2, TOK, DH)

    def attend(final, *arrays):
        return call(
            functools.partial(within_kernel, final),
            len(arrays),
            (shape(half, BF16), shape(half, F32)),
            [
                pltpu.VMEM((2, TOK, D), BF16),
                pltpu.VMEM((D, 2 * DH), BF16),
                pltpu.VMEM((2, 2, TOK, 2 * DH), BF16),
                pltpu.VMEM(half, BF16),
                pltpu.VMEM(half, F32),
                DMA((6,)),
                DMA((2, 2, 2)),
            ],
            3 * TOK * D * SLOTS * DH,
            5 << 20,
        )(*arrays)

    query_a, within_a = attend(False, own, other, pack_1, pack_2, kv0, kv1)

    chunks = total.reshape(CHIPS, SLOTS * DH // CHIPS, DH)
    chunks = lax.all_to_all(chunks, ("z", "x"), 0, 0, tiled=True)
    chunks, query_a = barrier((chunks, query_a))
    priors = call(prefix_kernel, 1, shape(chunks.shape, BF16), [], 1 << 16, 1 << 18, VMEM, 4)(chunks)
    prior = lax.all_to_all(priors, ("z", "x"), 0, 0, tiled=True).reshape(SLOTS, DH, DH)

    query_b, within_b = attend(True, own, other, pack_3, pack, pack_4, kv2, kv3)

    operands = (query_a, query_b, within_a, within_b, prior, s0, s1, s2, s3, norm_gain.reshape(DP, DH), pack_1, pack_2, pack_3, pack, pack_4)
    partial = []
    for block, kind, limit in ((1, BF16, 56), (0, BF16, 56)):
        partial.append(
            call(
                functools.partial(out_kernel, block),
                15,
                shape((TOK, D), kind),
                [
                    pltpu.VMEM((SLOTS, TOK, DH), BF16),
                    pltpu.VMEM((SLOTS, TOK, DH), F32),
                    pltpu.VMEM((SLOTS, DH, DH), BF16),
                    pltpu.VMEM((SLOTS, DH, DH), F32),
                    pltpu.VMEM((DP, DH), F32),
                    pltpu.VMEM((SLOTS, D, DH), BF16),
                    pltpu.VMEM((TOK, SLOTS * DH), BF16),
                    pltpu.VMEM((TOK, D), kind),
                    DMA((18,)),
                    DMA((4,)),
                ],
                5 << 28,
                5 << 20,
                HBM,
                limit,
            )(*operands)
        )
    got = lax.ppermute(partial[0], "core", SWAP)
    return (partial[1].astype(F32) + got.astype(F32)).astype(BF16)[None]


def solution(mesh):
    fine = Mesh(mesh.devices.reshape(DP, ZN, XN, 2), ("dp", "z", "x", "core"))
    seq = ("z", "x", "core")
    in_specs = (
        P("dp", seq, None),
        P(None, "dp"),
        P(None, "dp"),
        P(None, "dp"),
        P("dp", None),
        P(),
    )
    return jax.shard_map(body, mesh=fine, in_specs=in_specs, out_specs=P("dp", seq, None), check_vma=False)
```
